128 devices in a mesh: dp: 8 (over x_hi, z), tensor: 16 (over y, x_lo, core).
Axes of the slice: x: 4 (x_hi: 2, x_lo: 2; x = x_hi * 2 + x_lo), y: 4, z: 4, core: 2. Of those that a mesh axis runs over, the one named last changes fastest.
Arguments:
- cls_states: bfloat16 [4096, 5120], P(('dp', 'tensor')), may hold values from -6 to 6
- fc1_weight: bfloat16 [5120, 12800], P(None, 'tensor'), may hold values from -0.078125 to 0.078125
- fc2_weight: bfloat16 [12800, 5120], P('tensor'), may hold values from -0.0546875 to 0.0546875
- proj_weight: bfloat16 [5120, 1536], P('tensor'), may hold values from -0.078125 to 0.078125
- text_pooled: bfloat16 [4096, 1280], P(('dp', 'tensor')), may hold values from -6 to 6
- text_proj: bfloat16 [1280, 1536], replicated, may hold values from -0.15625 to 0.15625
- pair_owner: int32 [4096, 1], P(('dp', 'tensor')), may hold values from 0 to 7; in each aligned block of 32 rows (0 to 31, 32 to 63, ...) at most 8 rows name the same one
- pair_slot: int32 [4096], P(('dp', 'tensor')), may hold values from 0 to 31
- threshold: float32 [1], replicated, may hold values from -0.03 to 0.03
Outputs:
- filtered: bfloat16 [4096, 1536], P(('dp', 'tensor'))
- weight: float32 [4096], P(('dp', 'tensor'))
The draws below stay inside these ranges and needn't reach their ends.
Inputs may be any that keep to these rules, and one draw needn't show every extreme that they name: `pair_owner`: among the rows of one device, at most 8 images share an owner, and in some device exactly 8 do.
All inputs are finite; a program needn't handle non-finite values.
Results may differ from the reference program's by a relative error of at most 0.029.
Values may be sent and summed in bfloat16 or wider, within the bound.
No kernel may reach another device: no remote copies, remote signals or barrier semaphores. Data moves between devices by JAX's collectives and lax.ppermute only.
A program may use at most 128 MiB of HBM per device.

```python
import math
import jax
import jax.numpy as jnp
import numpy as np
from jax import lax

D = 5120
FF = 12800
E = 1536
TW = 1280
IMG_DEV = 32
TXT_DEV = 32
CAP = 8
IMAGES = 4096
TEXTS = 4096
N_DP = 8
N_TENSOR = 16


def touch_ends(entries, key, low, high):
    extent = entries.shape
    index_at = [jax.random.randint(jax.random.fold_in(key, axis), (), 0, extent[axis]) for axis in range(len(extent))]
    entries = entries.at[tuple(index_at)].set(low)
    longest = extent.index(max(extent))
    index_at[longest] = (index_at[longest] + 1) % extent[longest]
    return entries.at[tuple(index_at)].set(high)


def levels(rng, dims, split, smallest, high):
    def one(position, blocks):
        draws = jax.random.uniform(jax.random.fold_in(jax.random.fold_in(rng, 6), position), (blocks,), jnp.float32, smallest / len(split), high / len(split))
        return jnp.repeat(jnp.exp(draws), dims[position] // blocks).reshape((-1,) + (1,) * (len(dims) - position - 1))

    loudness = one(*split[0])
    for cut in split[1:]:
        loudness = loudness * one(*cut)
    return loudness


def deal_out(rng, own, number, rows, number_of, top, bound, slope):
    ranking = jax.random.permutation(rng, number_of)
    heavy_load, common = portions_of(number_of, rows * top, bound, slope, True), portions_of(number_of, rows * top, bound, slope, False)
    places = jnp.arange(number_of)

    def named(sizes, offset_by):
        used = int((sizes > 0).sum())
        fixed = max(1, used // 4)
        shifted = fixed + (places - fixed + offset_by * (used - fixed)) % max(1, number_of - fixed)
        return jnp.zeros((number_of,), jnp.int32).at[ranking[jnp.where(places < fixed, places, shifted)]].set(jnp.asarray(sizes, jnp.int32))

    sizes = jnp.where(number % 4 == 0, named(heavy_load, number // 4), named(common, number - number // 4 - 1))
    mixed = jax.random.permutation(jax.random.fold_in(own, 3), number_of)
    donor, taker = mixed[0:number_of // 2 * 2:2], mixed[1:number_of // 2 * 2:2]
    margin = jnp.minimum(sizes[donor] - 1, bound - sizes[taker]) // 2
    margin = jnp.where((donor == ranking[0]) | (taker == ranking[0]) | (sizes[taker] == 0), 0, jnp.maximum(margin, 0))
    shifted = jax.random.randint(jax.random.fold_in(own, 4), (number_of // 2,), 0, 1 << 20) % (margin + 1)
    sizes = sizes.at[donor].add(-shifted).at[taker].add(shifted)
    labels = jnp.searchsorted(jnp.cumsum(sizes), jnp.arange(rows * top), side="right").astype(jnp.int32)
    grid = labels.reshape(top, rows).T
    grid = grid[jax.random.permutation(jax.random.fold_in(own, 1), rows)]
    offset_by = jax.random.randint(jax.random.fold_in(own, 2), (rows, 1), 0, top)
    return jnp.take_along_axis(grid, (jnp.arange(top)[None, :] + offset_by) % top, axis=1)


def portions_of(count, total, most, lean, full):
    weights = [(1 << 20) // math.isqrt(standing ** lean) + 1 for standing in range(1, count + 1)]
    largest = most if full else min(most, max(-(-total // count), total * weights[0] // sum(weights)))
    least = 1 if total - largest >= count - 1 else 0
    counts, spare = [largest] + [least] * (count - 1), total - largest - least * (count - 1)
    while spare > 0:
        candidates = [i for i in range(1, count) if counts[i] < largest] or [i for i in range(1, count) if counts[i] < most]
        mass, remaining = sum([weights[i] for i in candidates]), spare
        for i in candidates:
            extra = min(most - counts[i], max(1, remaining * weights[i] // mass), spare)
            counts[i] = counts[i] + extra
            spare = spare - extra
    return np.array(counts)


def normal_values(key, extent, deviation, most, split=(), kind=jnp.bfloat16):
    drawn = jax.random.normal(key, extent, jnp.float32) * deviation
    if len(split) > 0:
        drawn = levels(key, extent, split, -0.22, 0.18) * drawn
    return jnp.clip(drawn, min=-most, max=most).astype(kind)


def setup_inputs(seed: int = 0) -> dict:
    streams_of = jax.random.split(jax.random.key(seed), 10)
    cls_states = normal_values(streams_of[0], (IMAGES, D), 1.0, 6.0, ((0, 128),))
    fc1_weight = normal_values(streams_of[1], (D, FF), D ** -0.5, 0.078125, ((1, 16),))
    fc2_weight = normal_values(streams_of[2], (FF, D), FF ** -0.5, 0.0546875, ((0, 16),))
    proj_weight = normal_values(streams_of[3], (D, E), D ** -0.5, 0.078125, ((0, 16),))
    text_pooled = normal_values(streams_of[4], (TEXTS, TW), 1.0, 6.0, ((0, 128),))
    text_proj = normal_values(streams_of[5], (TW, E), TW ** -0.5, 0.15625)
    pair_owner_keys = jax.random.split(jax.random.fold_in(streams_of[6], 1), IMAGES // IMG_DEV)
    pair_owner_turns = jax.random.permutation(jax.random.fold_in(streams_of[6], 3), IMAGES // IMG_DEV)
    pair_owner = jax.vmap(lambda own, number: deal_out(jax.random.fold_in(streams_of[6], 2), own, number, IMG_DEV, N_DP, 1, CAP, 1))(pair_owner_keys, pair_owner_turns).reshape((IMAGES, 1))
    pair_slot = touch_ends(jax.random.randint(streams_of[7], (IMAGES,), 0, TXT_DEV), jax.random.fold_in(streams_of[7], 1), 0, TXT_DEV - 1).astype(jnp.int32)
    threshold = jnp.clip(jax.random.uniform(streams_of[8], (1,), jnp.float32, -0.03, 0.03), -0.03, 0.03)
    return {"cls_states": cls_states, "fc1_weight": fc1_weight, "fc2_weight": fc2_weight, "proj_weight": proj_weight, "text_pooled": text_pooled, "text_proj": text_proj, "pair_owner": pair_owner, "pair_slot": pair_slot, "threshold": threshold}


eps = 1e-06
sharpness = 40.0

def layer_norm(values):
    average = lax.optimization_barrier(jnp.mean(values, axis=-1, keepdims=True))
    centred = values - average
    variance = lax.optimization_barrier(jnp.mean(centred * centred, axis=-1, keepdims=True))
    return centred * lax.rsqrt(variance + eps)

def reference(cls_states, fc1_weight, fc2_weight, proj_weight, text_pooled, text_proj, pair_owner, pair_slot, threshold):
    row_total = cls_states.shape[0]
    group_size = IMG_DEV * N_TENSOR
    groups = row_total // group_size
    hidden_cols = FF // N_TENSOR
    up_blocks = fc1_weight.reshape(D, N_TENSOR, hidden_cols).transpose(1, 0, 2)
    down_blocks = fc2_weight.reshape(N_TENSOR, hidden_cols, D)

    def one_group(group_rows):
        normed = layer_norm(group_rows.astype(jnp.float32)).astype(jnp.bfloat16)

        def add_partial(running, weights):
            w_up, w_down = weights
            hidden = jax.nn.gelu(jnp.dot(normed, w_up, preferred_element_type=jnp.float32), approximate=False).astype(jnp.bfloat16)
            partial_sum = jnp.dot(hidden, w_down, preferred_element_type=jnp.float32).astype(jnp.bfloat16)
            partial_sum = lax.optimization_barrier(partial_sum)
            return (running + partial_sum.astype(jnp.float32), None)
        start_value = jnp.zeros((group_rows.shape[0], D), jnp.float32)
        mlp_out, _ = lax.scan(add_partial, start_value, (up_blocks, down_blocks))
        final = layer_norm(group_rows.astype(jnp.float32) + mlp_out).astype(jnp.bfloat16)
        embedded = jnp.dot(final, proj_weight, preferred_element_type=jnp.float32)
        return embedded * lax.rsqrt(lax.optimization_barrier(jnp.sum(embedded * embedded, axis=-1, keepdims=True)) + eps)
    image_unit = lax.map(one_group, cls_states.reshape(groups, group_size, D)).reshape(row_total, E).astype(jnp.bfloat16)
    text_normed = layer_norm(text_pooled.astype(jnp.float32)).astype(jnp.bfloat16)
    text_embedded = jnp.dot(text_normed, text_proj, preferred_element_type=jnp.float32)
    text_unit = text_embedded * lax.rsqrt(lax.optimization_barrier(jnp.sum(text_embedded * text_embedded, axis=-1, keepdims=True)) + eps)
    image_index = jnp.arange(row_total, dtype=jnp.int32)
    tensor_index = image_index // IMG_DEV % N_TENSOR
    caption_index = ((pair_owner[:, 0] * N_TENSOR + tensor_index) * TXT_DEV + pair_slot).astype(jnp.int32)
    matched = text_unit[caption_index]
    cosine = lax.optimization_barrier(jnp.sum(image_unit.astype(jnp.float32) * matched, axis=-1))
    weight = jax.nn.sigmoid(sharpness * (cosine - threshold[0]))
    filtered = (weight[:, None] * image_unit.astype(jnp.float32)).astype(jnp.bfloat16)
    return (filtered, weight)
```

```python
import functools

import jax
import jax.numpy as jnp
from jax import lax
from jax.experimental import pallas as pl
from jax.experimental.pallas import tpu as pltpu
from jax.sharding import PartitionSpec as P

eps = 1e-06
sharpness = 40.0
AXES = ("dp", "tensor")
BLK = 640
EW = 1536 + 128
f32 = jnp.float32
bf16 = jnp.bfloat16


def moves(dx=0, dy=0, mz=0, flip=False):
    def place(x, y, z, c):
        return ((x // 2) * 4 + z) * 16 + y * 4 + (x % 2) * 2 + c

    return [
        (place(x, y, z, c), place((x + dx) % 4, (y + dy) % 4, z ^ mz, c ^ int(flip)))
        for x in range(4)
        for y in range(4)
        for z in range(4)
        for c in range(2)
    ]


def shift(value, **step):
    return lax.ppermute(value, AXES, moves(**step))


def after(value, *others):
    return lax.optimization_barrier((value,) + others)[0]


NT = (((1,), (1,)), ((), ()))
TN = (((0,), (0,)), ((), ()))
VM = pl.BlockSpec(memory_space=pltpu.VMEM)
SM = pl.BlockSpec(memory_space=pltpu.SMEM)
HB = pl.BlockSpec(memory_space=pltpu.HBM)
HALF = 4 * BLK


def struct(shape, dtype):
    return jax.ShapeDtypeStruct(shape, dtype)


def call(body, scalars, arrays, outs, scratch=(), remote=0, limit=12, away=False, size=1024):
    inside = len(arrays) - remote
    return pl.pallas_call(
        body,
        in_specs=[SM] * len(scalars) + [VM] * inside + [HB] * remote,
        out_specs=((HB if away else VM),) * len(outs),
        out_shape=outs,
        scratch_shapes=scratch,
        compiler_params=pltpu.CompilerParams(vmem_limit_bytes=limit * 1024 * 1024),
        cost_estimate=pl.CostEstimate(flops=1024, bytes_accessed=size, transcendentals=0),
    )(*scalars, *arrays)


def norm_kernel(cls_ref, normed_ref, r_ref, l_ref, centred_ref):
    values = cls_ref[...].astype(f32)
    centred = values - jnp.mean(values, axis=-1, keepdims=True)
    variance = jnp.mean(centred * centred, axis=-1, keepdims=True)
    centred_ref[...] = centred
    normed = (centred * lax.rsqrt(variance + eps)).astype(bf16)
    normed_ref[...] = normed
    r_ref[...] = normed[:16]
    l_ref[...] = normed[16:]


def norm_call(cls_states):
    width = cls_states.shape[1]
    outs = (struct((32, width), bf16), struct((16, width), bf16), struct((16, width), bf16), struct((32, width), f32))
    return call(norm_kernel, (), (cls_states,), outs)


def halves_kernel(*refs):
    *ins, r_ref, l_ref = refs
    for k, ref in enumerate(ins):
        r_ref[16 * k : 16 * k + 16] = ref[:16]
        l_ref[16 * k : 16 * k + 16] = ref[16:]


def halves_call(*ins):
    outs = (struct((16 * len(ins), ins[0].shape[1]), bf16),) * 2
    return call(halves_kernel, (), ins, outs)


def prep_kernel(parity, f_ref, a_ref, b_ref, means, sems):
    copies = []
    for k in range(4):
        for half, out in ((1 - parity[0], a_ref), (parity[0], b_ref)):
            at = pl.ds(pl.multiple_of((2 * k + half) * BLK, 128), BLK)
            sem = sems.at[len(copies)]
            copies.append(pltpu.make_async_copy(f_ref.at[:, at], out.at[:, pl.ds(k * BLK, BLK)], sem))
    start(copies)
    mean = jnp.sum(f_ref[...].astype(f32), axis=-1, keepdims=True) / f_ref.shape[1]
    high = mean.astype(bf16).astype(f32)
    lane = lax.broadcasted_iota(jnp.int32, means.shape, 1)
    means[...] = jnp.where(lane == 0, high, jnp.where(lane == 1, mean - high, 0.0)).astype(bf16)
    last = pltpu.make_async_copy(means, a_ref.at[:, pl.ds(HALF, 128)], sems.at[8])
    last.start()
    wait(copies)
    last.wait()


def prep_call(parity, f):
    rows = f.shape[0]
    return call(
        prep_kernel,
        (parity,),
        (f,),
        (struct((rows, HALF + 128), bf16), struct((rows, HALF), bf16)),
        scratch=[pltpu.VMEM((rows, 128), bf16), pltpu.SemaphoreType.DMA((9,))],
        away=True,
        size=16 * 1024 * 1024,
    )


def fetch(f_ref, o_ref, cols, first, buf, sems):
    copies = []
    for q in range(2):
        at = pl.ds(pl.multiple_of(cols[first + q] // 2 * BLK, 128), BLK)
        for k, ref in enumerate((f_ref, o_ref)):
            to = buf.at[pl.ds(800 * k, 800), pl.ds(BLK * q, BLK)]
            copies.append(pltpu.make_async_copy(ref.at[:, at], to, sems.at[2 * q + k]))
    return copies


def start(copies):
    for copy in copies:
        copy.start()


def wait(copies):
    for copy in copies:
        copy.wait()


def fc2_pair(cols, first, h_ref, mean_ref, buf, res_ref):
    pair = lax.dot_general(h_ref[...], buf[...], TN, preferred_element_type=f32)
    for q in range(2):
        part = pair[:, BLK * q : BLK * q + BLK] - mean_ref[:, :1]
        res = res_ref[:, pl.ds(pl.multiple_of(cols[first + q] * BLK, 128), BLK)]
        upper = jnp.concatenate([part[0:16] + res[0:16], part[16:128]], axis=0)
        lower = jnp.concatenate([part[128:192], part[192:208] + res[16:32], part[208:256]], axis=0)
        yield q, upper, lower


def first_kernel(cols, *refs):
    (n0, n1, n2, n3, a0, a13, a2, b0, b13, b2, res_ref, w_ref, v_ref, f_ref, o_ref) = refs[:15]
    h_ref, mean_ref, to_r, to_l, rows, wbuf, fbuf, mbuf, sems, fsems = refs[15:]
    spans = ((0, w_ref, 0, 160), (160, w_ref, 160, 640), (800, v_ref, 0, 400), (1200, v_ref, 400, 400))
    loads = [
        pltpu.make_async_copy(ref.at[pl.ds(at, size)], wbuf.at[pl.ds(base, size)], sems.at[k])
        for k, (base, ref, at, size) in enumerate(spans)
    ]
    columns = fetch(f_ref, o_ref, cols, 0, fbuf, fsems) + [
        pltpu.make_async_copy(ref.at[:, pl.ds(HALF, 128)], mbuf.at[pl.ds(800 * k, 800)], fsems.at[4 + k])
        for k, ref in enumerate((f_ref, o_ref))
    ]
    loads[0].start()
    loads[1].start()
    own = (n0, n1, n2, n3)
    for k in range(4):
        rows[16 * k : 16 * k + 16] = own[k][0:16]
        rows[192 + 16 * k : 208 + 16 * k] = own[k][16:32]
    for base, (p0, p13, p2) in ((64, (b0, b13, b2)), (128, (a0, a13, a2))):
        rows[base : base + 16] = p0[...]
        rows[base + 16 : base + 32] = p13[0:16]
        rows[base + 32 : base + 48] = p2[...]
        rows[base + 48 : base + 64] = p13[16:32]
    for k, (base, _, _, size) in enumerate(spans):
        loads[k].wait()
        if k < 2:
            loads[k + 2].start()
        if k == 2:
            start(columns)
        z = lax.dot_general(wbuf[base : base + size], rows[...], NT, preferred_element_type=f32)
        act = 0.5 * z * (1.0 + lax.erf(z * (0.5**0.5)))
        h_ref[base : base + size] = act.astype(bf16)
    wait(columns)
    means = lax.dot_general(h_ref[...], mbuf[...], TN, preferred_element_type=f32)
    mean_ref[...] = jnp.broadcast_to(jnp.sum(means, axis=-1, keepdims=True), mean_ref.shape)
    for q, upper, lower in fc2_pair(cols, 0, h_ref, mean_ref, fbuf, res_ref):
        to_r[q] = upper.astype(bf16)
        to_l[q] = lower.astype(bf16)


def first_call(cols, pieces, centred, w, v, f, o):
    outs = (
        struct((1600, 256), bf16),
        struct((256, 128), f32),
        struct((2, 128, BLK), bf16),
        struct((2, 128, BLK), bf16),
    )
    return call(
        first_kernel,
        (cols,),
        (*pieces, centred, w, v, f, o),
        outs,
        scratch=[
            pltpu.VMEM((256, w.shape[1]), bf16),
            pltpu.VMEM((1600, w.shape[1]), bf16),
            pltpu.VMEM((1600, 2 * BLK), bf16),
            pltpu.VMEM((1600, 128), bf16),
            pltpu.SemaphoreType.DMA((4,)),
            pltpu.SemaphoreType.DMA((6,)),
        ],
        remote=4,
        limit=52,
    )


def second_kernel(cols, h_ref, mean_ref, res_ref, f_ref, o_ref, fb_ref, ob_ref, to_r, to_l, own_ref, fbuf, sems):
    loads = [fetch(f_ref, o_ref, cols, 0, fbuf.at[0], sems.at[0])] + [
        fetch(fb_ref, ob_ref, cols, 2 * k, fbuf.at[k], sems.at[k]) for k in (1, 2)
    ]
    start(loads[0])
    start(loads[1])
    for k in range(3):
        wait(loads[k])
        if k == 0:
            start(loads[2])
        for q, upper, lower in fc2_pair(cols, 2 * k, h_ref, mean_ref, fbuf.at[k], res_ref):
            if k == 0:
                to_r[q] = upper.astype(bf16)
                to_l[q] = lower.astype(bf16)
            else:
                own_ref[2 * k - 2 + q, 0:128] = upper
                own_ref[2 * k - 2 + q, 128:256] = lower


def second_call(cols, h, h_mean, centred, f, o, fb, ob):
    outs = (struct((2, 128, BLK), bf16), struct((2, 128, BLK), bf16), struct((4, 256, BLK), f32))
    return call(
        second_kernel,
        (cols,),
        (h, h_mean, centred, f, o, fb, ob),
        outs,
        scratch=[pltpu.VMEM((3, 1600, 2 * BLK), bf16), pltpu.SemaphoreType.DMA((3, 4))],
        remote=4,
        limit=40,
    )


def add_kernel(place, own_ref, up_ref, low_ref, *outs):
    for k, out in enumerate(outs):
        out[0:128] = (own_ref[place + k, :128] + up_ref[k].astype(f32)).astype(bf16)
        out[128:256] = (own_ref[place + k, 128:] + low_ref[k].astype(f32)).astype(bf16)


def add_call(place, count, own, up, low):
    outs = (struct((256, BLK), bf16),) * count
    return call(functools.partial(add_kernel, place), (), (own, up, low), outs)


def proj_kernel(core, own_ref, up_ref, low_ref, t1, t2, t3, w_ref, o_ref, home_ref, a_ref, b_ref, total, weight):
    weight[pl.ds(pl.multiple_of(core[0] * 320, 64), 320)] = w_ref[...]
    weight[pl.ds(pl.multiple_of((1 - core[0]) * 320, 64), 320)] = o_ref[...]
    total[0:128] = own_ref[3, :128] + up_ref[1].astype(f32)
    total[128:256] = own_ref[3, 128:] + low_ref[1].astype(f32)
    for k, got in ((1, t1), (2, t2), (3, t3)):
        for group in range(4):
            for j in range(4):
                mine = 64 * group + 16 * ((j - k) % 4)
                theirs = 64 * group + 16 * j
                total[mine : mine + 16] += got[theirs : theirs + 16].astype(f32)
    x = total[...]
    squares = jnp.sum(x * x, axis=-1, keepdims=True)
    high = squares.astype(bf16).astype(f32)
    lane = lax.broadcasted_iota(jnp.int32, (256, 128), 1)
    extra = jnp.where(lane == 0, high, jnp.where(lane == 1, squares - high, 0.0)).astype(bf16)
    e = jnp.dot(x.astype(bf16), weight[...], preferred_element_type=f32).astype(bf16)
    for k in range(4):
        for at, base in ((0, 0), (16, 192)):
            src = slice(base + 16 * k, base + 16 * k + 16)
            home_ref[k, at : at + 16, :1536] = e[src]
            home_ref[k, at : at + 16, 1536:] = extra[src]
    b_ref[:, :1536] = e[64:128]
    b_ref[:, 1536:] = extra[64:128]
    a_ref[:, :1536] = e[128:192]
    a_ref[:, 1536:] = extra[128:192]


def proj_call(core, own, up, low, ts, w, o):
    outs = (struct((4, 32, EW), bf16), struct((64, EW), bf16), struct((64, EW), bf16))
    return call(
        proj_kernel,
        (core,),
        (own, up, low, *ts, w, o),
        outs,
        scratch=[pltpu.VMEM((256, BLK), f32), pltpu.VMEM((BLK, 1536), bf16)],
    )


def pair_kernel(home_ref, r_ref, l_ref, s0, s1, s2, s3):
    for k, out in enumerate((s0, s1, s2, s3)):
        at = slice(16 * k, 16 * k + 16)
        out[0:16] = (home_ref[k, 0:16].astype(f32) + r_ref[at].astype(f32)).astype(out.dtype)
        out[16:32] = (home_ref[k, 16:32].astype(f32) + l_ref[at].astype(f32)).astype(out.dtype)


def pair_call(home, r, l):
    outs = (struct((32, EW), f32),) + (struct((32, EW), bf16),) * 3
    return call(pair_kernel, (), (home, r, l), outs)


def text_kernel(index_ref, pooled_ref, proj_ref, out_ref):
    count = pooled_ref.shape[0]
    lane = lax.broadcasted_iota(jnp.int32, (32, count), 1)
    picker = jnp.where(lane == index_ref[...], 1.0, 0.0).astype(bf16)
    values = jnp.dot(picker, pooled_ref[...], preferred_element_type=f32)
    centred = values - jnp.mean(values, axis=-1, keepdims=True)
    variance = jnp.mean(centred * centred, axis=-1, keepdims=True)
    normed = (centred * lax.rsqrt(variance + eps)).astype(bf16)
    u = jnp.dot(normed, proj_ref[...], preferred_element_type=f32)
    out_ref[...] = u * lax.rsqrt(jnp.sum(u * u, axis=-1, keepdims=True) + eps)


def text_call(index, pooled, text_proj):
    outs = (struct((32, text_proj.shape[1]), f32),)
    return call(
        text_kernel, (), (index, pooled, text_proj), outs
    )[0]


def last_kernel(threshold_ref, s0, s1, s2, s3, text_ref, filtered_ref, weight_ref):
    total = s0[...] + s1[...].astype(f32) + s2[...].astype(f32) + s3[...].astype(f32)
    squares = jnp.sum(total[:, 1536:], axis=-1, keepdims=True)
    scale = lax.rsqrt(squares / 5120.0 + eps)
    e = total[:, :1536] * scale
    unit = (e * lax.rsqrt(jnp.sum(e * e, axis=-1, keepdims=True) + eps)).astype(bf16).astype(f32)
    cosine = jnp.sum(unit * text_ref[...], axis=-1, keepdims=True)
    weight = jax.nn.sigmoid(sharpness * (cosine - threshold_ref[0]))
    filtered_ref[...] = (weight * unit).astype(bf16)
    row = lax.broadcasted_iota(jnp.int32, (32, 32), 0)
    column = lax.broadcasted_iota(jnp.int32, (32, 32), 1)
    weight_ref[...] = jnp.sum(jnp.where(row == column, weight, 0.0), axis=0, keepdims=True)


def last_call(parts, text, threshold):
    outs = (struct((32, 1536), bf16), struct((1, 32), f32))
    return call(last_kernel, (threshold,), (*parts, text), outs)


def shards(
    cls_states, fc1_weight, fc2_weight, proj_weight, text_pooled, text_proj, pair_owner, pair_slot, threshold
):
    d = lax.axis_index("dp")
    t = lax.axis_index("tensor")
    x_hi, z, y, x_lo, core = d // 4, d % 4, t // 4, (t // 2) % 2, t % 2

    fc1_rows = fc1_weight.T

    fc1_other = shift(fc1_rows, flip=True)
    normed, r0, l0, centred = norm_call(cls_states)
    n1, n3 = shift(normed, dy=-1), shift(normed, dy=1)
    a0, b0 = shift(r0, dx=1), shift(l0, dx=-1)
    fc2_a, fc2_b = prep_call(x_lo.astype(jnp.int32).reshape(1), fc2_weight)
    n2 = shift(after(normed, a0, b0, fc2_a), dy=2)
    tz = after(text_pooled, a0, b0, fc2_a)
    tz = jnp.concatenate([tz, shift(tz, mz=1)])
    tz = jnp.concatenate([tz, shift(tz, mz=2)])
    fc2_a_other = shift(after(fc2_a, tz), flip=True)
    r13, l13 = halves_call(n1, n3)
    a13, b13 = shift(r13, dx=1), shift(l13, dx=-1)
    r2, l2 = halves_call(n2)
    a2, b2 = shift(r2, dx=1), shift(l2, dx=-1)
    fc2_b_other = shift(after(fc2_b, a13, b13, a2, b2), flip=True)
    pooled = jnp.concatenate([tz, shift(after(tz, a13, b13, a2, b2), dx=2)])

    def blocks(parity, *ks):
        return [2 * ((y + k) % 4) + parity for k in ks]

    pieces = (normed, n1, n2, n3, a0, a13, a2, b0, b13, b2)
    cols = jnp.stack(blocks(1 - x_lo, 1, 3)).astype(jnp.int32)
    h, h_mean, to_r, to_l = first_call(cols, pieces, centred, fc1_rows, fc1_other, fc2_a, fc2_a_other)
    got_r, got_l = shift(to_l, dx=-1), shift(to_r, dx=1)
    proj_other = shift(after(proj_weight, h), flip=True)
    cols = jnp.stack(blocks(1 - x_lo, 2, 0) + blocks(x_lo, 1, 3, 2, 0)).astype(jnp.int32)
    to_r2, to_l2, own = second_call(cols, h, h_mean, centred, fc2_a, fc2_a_other, fc2_b, fc2_b_other)
    got_r2, got_l2 = shift(to_l2, dx=-1), shift(to_r2, dx=1)
    s1, s3 = add_call(0, 2, own, got_r, got_l)
    t1, t3 = shift(s1, dy=1), shift(s3, dy=-1)
    (s2,) = add_call(2, 1, own, got_r2, got_l2)
    t2 = shift(s2, dy=2)

    owner = pair_owner[:, 0]
    relative = ((owner // 4) ^ x_hi) * 4 + ((owner % 4) ^ z)
    index = (relative * 32 + pair_slot).reshape(32, 1)
    text = text_call(after(index, s2), pooled, text_proj)

    core_index = core.astype(jnp.int32).reshape(1)
    home, e_a, e_b = proj_call(
        core_index, own, got_r2, got_l2, (t1, t2, t3), after(proj_weight, text), proj_other
    )
    s0, s1, s2, s3 = pair_call(home, shift(e_a, dx=-1), shift(e_b, dx=1))
    parts = (s0, shift(s1, dy=1), shift(s2, dy=2), shift(s3, dy=3))
    filtered, weight = last_call(parts, text, threshold)
    return filtered, weight.reshape(32)


def solution(mesh):
    placed = (
        P(("dp", "tensor"), None),
        P(None, "tensor"),
        P("tensor", None),
        P("tensor", None),
        P(("dp", "tensor"), None),
        P(),
        P(("dp", "tensor"), None),
        P(("dp", "tensor")),
        P(),
    )
    return jax.shard_map(
        shards,
        mesh=mesh,
        in_specs=placed,
        out_specs=(P(("dp", "tensor"), None), P(("dp", "tensor"))),
        check_vma=False,
    )
```

```python
import functools

import jax
import jax.numpy as jnp
from jax import lax
from jax.experimental import pallas as pl
from jax.experimental.pallas import tpu as pltpu
from jax.sharding import PartitionSpec as P

eps = 1e-06
sharpness = 40.0
AXES = ("dp", "tensor")
BLK = 640
EW = 1536 + 128
f32 = jnp.float32
bf16 = jnp.bfloat16


def moves(dx=0, dy=0, mz=0, flip=False):
    def place(x, y, z, c):
        return ((x // 2) * 4 + z) * 16 + y * 4 + (x % 2) * 2 + c

    return [
        (place(x, y, z, c), place((x + dx) % 4, (y + dy) % 4, z ^ mz, c ^ int(flip)))
        for x in range(4)
        for y in range(4)
        for z in range(4)
        for c in range(2)
    ]


def shift(value, **step):
    return lax.ppermute(value, AXES, moves(**step))


def after(value, *others):
    return lax.optimization_barrier((value,) + others)[0]


NT = (((1,), (1,)), ((), ()))
TN = (((0,), (0,)), ((), ()))
VM = pl.BlockSpec(memory_space=pltpu.VMEM)
SM = pl.BlockSpec(memory_space=pltpu.SMEM)
HB = pl.BlockSpec(memory_space=pltpu.HBM)


def struct(shape, dtype):
    return jax.ShapeDtypeStruct(shape, dtype)


def call(body, scalars, arrays, outs, scratch=(), remote=0, limit=12, size=1024):
    inside = len(arrays) - remote
    return pl.pallas_call(
        body,
        in_specs=[SM] * len(scalars) + [VM] * inside + [HB] * remote,
        out_specs=(VM,) * len(outs),
        out_shape=outs,
        scratch_shapes=scratch,
        compiler_params=pltpu.CompilerParams(vmem_limit_bytes=limit * 1024 * 1024),
        cost_estimate=pl.CostEstimate(flops=1024, bytes_accessed=size, transcendentals=0),
    )(*scalars, *arrays)


def norm_kernel(cls_ref, normed_ref, centred_ref):
    values = cls_ref[...].astype(f32)
    centred = values - jnp.mean(values, axis=-1, keepdims=True)
    variance = jnp.mean(centred * centred, axis=-1, keepdims=True)
    centred_ref[...] = centred
    normed_ref[...] = (centred * lax.rsqrt(variance + eps)).astype(bf16)


def norm_call(cls_states):
    outs = (struct(cls_states.shape, bf16), struct(cls_states.shape, f32))
    return call(norm_kernel, (), (cls_states,), outs)


def halves_kernel(n0, n1, n2, n3, r_ref, l_ref):
    for k, ref in enumerate((n0, n1, n2, n3)):
        r_ref[16 * k : 16 * k + 16] = ref[:16]
        l_ref[16 * k : 16 * k + 16] = ref[16:]


def halves_call(*ins):
    outs = (struct((64, ins[0].shape[1]), bf16),) * 2
    return call(halves_kernel, (), ins, outs)


def mean_kernel(f_ref, out_ref):
    mean = jnp.sum(f_ref[...].astype(f32), axis=-1, keepdims=True) / f_ref.shape[1]
    high = mean.astype(bf16).astype(f32)
    lane = lax.broadcasted_iota(jnp.int32, out_ref.shape, 1)
    out_ref[...] = jnp.where(lane == 0, high, jnp.where(lane == 1, mean - high, 0.0)).astype(bf16)


def mean_call(f):
    return call(mean_kernel, (), (f,), (struct((f.shape[0], 128), bf16),), size=16 * 1024 * 1024)[0]


def start(copies):
    for copy in copies:
        copy.start()


def wait(copies):
    for copy in copies:
        copy.wait()


def stage_kernel(w_ref, v_ref, out_ref, sems):
    copies = [
        pltpu.make_async_copy(ref.at[pl.ds(at, 400)], out_ref.at[pl.ds(base + at, 400)], sems.at[(base + at) // 400])
        for base, ref in ((0, w_ref), (800, v_ref))
        for at in (0, 400)
    ]
    start(copies)
    wait(copies)


def stage_call(w, v):
    outs = (struct((1600, w.shape[1]), bf16),)
    return call(
        stage_kernel, (), (w, v), outs, [pltpu.SemaphoreType.DMA((4,))], remote=2, limit=4, size=32 * 1024 * 1024
    )[0]


def columns_kernel(cols, f_ref, o_ref, out_ref, sems):
    copies = []
    for q in range(4):
        at = pl.ds(pl.multiple_of(cols[q] * BLK, 128), BLK)
        for k, ref in enumerate((f_ref, o_ref)):
            to = out_ref.at[pl.ds(800 * k, 800), pl.ds(BLK * q, BLK)]
            copies.append(pltpu.make_async_copy(ref.at[:, at], to, sems.at[2 * q + k]))
    start(copies)
    wait(copies)


def columns_call(cols, f, o):
    outs = (struct((1600, 4 * BLK), bf16),)
    return call(
        columns_kernel, (cols,), (f, o), outs, [pltpu.SemaphoreType.DMA((8,))], remote=2, limit=4, size=16 * 1024 * 1024
    )[0]


def fc2_pair(cols, first, h_ref, mean_ref, f_ref, res_ref):
    pair = lax.dot_general(h_ref[...], f_ref[:, BLK * first : BLK * first + 2 * BLK], TN, preferred_element_type=f32)
    for q in range(2):
        part = pair[:, BLK * q : BLK * q + BLK] - mean_ref[:, :1]
        res = res_ref[:, pl.ds(pl.multiple_of(cols[first + q] * BLK, 128), BLK)]
        upper = jnp.concatenate([part[0:16] + res[0:16], part[16:128]], axis=0)
        lower = jnp.concatenate([part[128:192], part[192:208] + res[16:32], part[208:256]], axis=0)
        yield q, upper, lower


def fc1_kernel(w_ref, wm_ref, vm_ref, r, b, a, l, h_ref, mean_ref, rows, sems):
    parts = [pltpu.make_async_copy(ref, rows.at[pl.ds(64 * k, 64)], sems.at[k]) for k, ref in enumerate((r, b, a, l))]
    start(parts)
    wait(parts)
    for at in range(0, 1600, 400):
        z = lax.dot_general(w_ref[at : at + 400], rows[...], NT, preferred_element_type=f32)
        act = 0.5 * z * (1.0 + lax.erf(z * (0.5**0.5)))
        h_ref[at : at + 400] = act.astype(bf16)
    means = lax.dot_general(h_ref[0:800], wm_ref[...], TN, preferred_element_type=f32) + lax.dot_general(
        h_ref[800:1600], vm_ref[...], TN, preferred_element_type=f32
    )
    mean_ref[...] = jnp.broadcast_to(jnp.sum(means, axis=-1, keepdims=True), mean_ref.shape)


def fc1_call(rows, w, w_mean, v_mean):
    outs = (struct((1600, 256), bf16), struct((256, 128), f32))
    return call(
        fc1_kernel,
        (),
        (w, w_mean, v_mean, *rows),
        outs,
        scratch=[pltpu.VMEM((256, w.shape[1]), bf16), pltpu.SemaphoreType.DMA((4,))],
        remote=4,
        limit=10,
    )


def away_kernel(cols, h_ref, mean_ref, res_ref, f_ref, *outs):
    for k in range(2):
        for q, upper, lower in fc2_pair(cols, 2 * k, h_ref, mean_ref, f_ref, res_ref):
            outs[2 * k][q] = upper.astype(bf16)
            outs[2 * k + 1][q] = lower.astype(bf16)


def away_call(cols, h, h_mean, centred, f):
    outs = (struct((2, 128, BLK), bf16),) * 4
    return call(away_kernel, (cols,), (h, h_mean, centred, f), outs, limit=20)


def own_kernel(cols, h_ref, mean_ref, res_ref, f_ref, o_ref, own_ref, buf, sems):
    loads = []
    for q in range(4):
        at = pl.ds(pl.multiple_of(cols[q] * BLK, 128), BLK)
        for k, ref in enumerate((f_ref, o_ref)):
            to = buf.at[pl.ds(800 * k, 800), pl.ds(BLK * q, BLK)]
            loads.append(pltpu.make_async_copy(ref.at[:, at], to, sems.at[2 * q + k]))
    start(loads[:4])
    for k in range(2):
        wait(loads[4 * k : 4 * k + 4])
        if k == 0:
            start(loads[4:])
        for q, upper, lower in fc2_pair(cols, 2 * k, h_ref, mean_ref, buf, res_ref):
            own_ref[2 * k + q, 0:128] = upper
            own_ref[2 * k + q, 128:256] = lower


def own_call(cols, h, h_mean, centred, f, o):
    return call(
        own_kernel,
        (cols,),
        (h, h_mean, centred, f, o),
        (struct((4, 256, BLK), f32),),
        scratch=[pltpu.VMEM((1600, 4 * BLK), bf16), pltpu.SemaphoreType.DMA((8,))],
        remote=2,
        limit=29,
        size=16 * 1024 * 1024,
    )[0]


def add_kernel(place, own_ref, up_ref, low_ref, *outs):
    for k, out in enumerate(outs):
        out[0:128] = (own_ref[place + k, :128] + up_ref[k].astype(f32)).astype(bf16)
        out[128:256] = (own_ref[place + k, 128:] + low_ref[k].astype(f32)).astype(bf16)


def add_call(place, count, own, up, low):
    outs = (struct((256, BLK), bf16),) * count
    return call(functools.partial(add_kernel, place), (), (own, up, low), outs)


def proj_kernel(core, own_ref, up_ref, low_ref, t1, t2, t3, w_ref, o_ref, home_ref, a_ref, b_ref, total, weight):
    weight[pl.ds(pl.multiple_of(core[0] * 320, 64), 320)] = w_ref[...]
    weight[pl.ds(pl.multiple_of((1 - core[0]) * 320, 64), 320)] = o_ref[...]
    total[0:128] = own_ref[3, :128] + up_ref[1].astype(f32)
    total[128:256] = own_ref[3, 128:] + low_ref[1].astype(f32)
    for k, got in ((1, t1), (2, t2), (3, t3)):
        for group in range(4):
            for j in range(4):
                mine = 64 * group + 16 * ((j - k) % 4)
                theirs = 64 * group + 16 * j
                total[mine : mine + 16] += got[theirs : theirs + 16].astype(f32)
    x = total[...]
    squares = jnp.sum(x * x, axis=-1, keepdims=True)
    high = squares.astype(bf16).astype(f32)
    lane = lax.broadcasted_iota(jnp.int32, (256, 128), 1)
    extra = jnp.where(lane == 0, high, jnp.where(lane == 1, squares - high, 0.0)).astype(bf16)
    e = jnp.dot(x.astype(bf16), weight[...], preferred_element_type=f32).astype(bf16)
    for k in range(4):
        for at, base in ((0, 0), (16, 192)):
            src = slice(base + 16 * k, base + 16 * k + 16)
            home_ref[k, at : at + 16, :1536] = e[src]
            home_ref[k, at : at + 16, 1536:] = extra[src]
    b_ref[:, :1536] = e[64:128]
    b_ref[:, 1536:] = extra[64:128]
    a_ref[:, :1536] = e[128:192]
    a_ref[:, 1536:] = extra[128:192]


def proj_call(core, own, up, low, ts, w, o):
    outs = (struct((4, 32, EW), bf16), struct((64, EW), bf16), struct((64, EW), bf16))
    return call(
        proj_kernel,
        (core,),
        (own, up, low, *ts, w, o),
        outs,
        scratch=[pltpu.VMEM((256, BLK), f32), pltpu.VMEM((BLK, 1536), bf16)],
    )


def pair_kernel(home_ref, r_ref, l_ref, s0, s1, s2, s3):
    for k, out in enumerate((s0, s1, s2, s3)):
        at = slice(16 * k, 16 * k + 16)
        out[0:16] = (home_ref[k, 0:16].astype(f32) + r_ref[at].astype(f32)).astype(out.dtype)
        out[16:32] = (home_ref[k, 16:32].astype(f32) + l_ref[at].astype(f32)).astype(out.dtype)


def pair_call(home, r, l):
    outs = (struct((32, EW), f32),) + (struct((32, EW), bf16),) * 3
    return call(pair_kernel, (), (home, r, l), outs)


def text_kernel(index_ref, pooled_ref, proj_ref, out_ref):
    count = pooled_ref.shape[0]
    lane = lax.broadcasted_iota(jnp.int32, (32, count), 1)
    picker = jnp.where(lane == index_ref[...], 1.0, 0.0).astype(bf16)
    values = jnp.dot(picker, pooled_ref[...], preferred_element_type=f32)
    centred = values - jnp.mean(values, axis=-1, keepdims=True)
    variance = jnp.mean(centred * centred, axis=-1, keepdims=True)
    normed = (centred * lax.rsqrt(variance + eps)).astype(bf16)
    u = jnp.dot(normed, proj_ref[...], preferred_element_type=f32)
    out_ref[...] = u * lax.rsqrt(jnp.sum(u * u, axis=-1, keepdims=True) + eps)


def text_call(index, pooled, text_proj):
    outs = (struct((32, text_proj.shape[1]), f32),)
    return call(
        text_kernel, (), (index, pooled, text_proj), outs
    )[0]


def last_kernel(threshold_ref, s0, s1, s2, s3, text_ref, filtered_ref, weight_ref):
    total = s0[...] + s1[...].astype(f32) + s2[...].astype(f32) + s3[...].astype(f32)
    squares = jnp.sum(total[:, 1536:], axis=-1, keepdims=True)
    scale = lax.rsqrt(squares / 5120.0 + eps)
    e = total[:, :1536] * scale
    unit = (e * lax.rsqrt(jnp.sum(e * e, axis=-1, keepdims=True) + eps)).astype(bf16).astype(f32)
    cosine = jnp.sum(unit * text_ref[...], axis=-1, keepdims=True)
    weight = jax.nn.sigmoid(sharpness * (cosine - threshold_ref[0]))
    filtered_ref[...] = (weight * unit).astype(bf16)
    row = lax.broadcasted_iota(jnp.int32, (32, 32), 0)
    column = lax.broadcasted_iota(jnp.int32, (32, 32), 1)
    weight_ref[...] = jnp.sum(jnp.where(row == column, weight, 0.0), axis=0, keepdims=True)


def last_call(parts, text, threshold):
    outs = (struct((32, 1536), bf16), struct((1, 32), f32))
    return call(last_kernel, (threshold,), (*parts, text), outs)


def shards(
    cls_states, fc1_weight, fc2_weight, proj_weight, text_pooled, text_proj, pair_owner, pair_slot, threshold
):
    d = lax.axis_index("dp")
    t = lax.axis_index("tensor")
    x_hi, z, y, x_lo, core = d // 4, d % 4, t // 4, (t // 2) % 2, t % 2

    fc1_rows = fc1_weight.T

    fc1_other = shift(fc1_rows, flip=True)
    normed, centred = norm_call(cls_states)
    n1, n3, n2 = shift(normed, dy=-1), shift(normed, dy=1), shift(normed, dy=2)
    pooled = jnp.concatenate([text_pooled, shift(text_pooled, dx=2)])
    w_mean = mean_call(fc2_weight)
    r, l = halves_call(normed, n1, after(n2, w_mean, pooled), n3)
    a, b = shift(r, dx=1), shift(l, dx=-1)
    fc2_other = shift(after(fc2_weight, r), flip=True)
    v_mean = shift(after(w_mean, r), flip=True)
    proj_other = shift(after(proj_weight, r), flip=True)
    fc1_both = stage_call(after(fc1_rows, r), fc1_other)

    def blocks(parity, *ks):
        return jnp.stack([2 * ((y + k) % 4) + parity for k in ks]).astype(jnp.int32)

    cols = blocks(1 - x_lo, 1, 3, 2, 0)
    fc2_both = columns_call(cols, fc2_weight, fc2_other)
    h, h_mean = fc1_call((r, after(b, fc2_both, proj_other), a, l), fc1_both, w_mean, v_mean)
    to_r, to_l, to_r2, to_l2 = away_call(cols, h, h_mean, centred, fc2_both)
    got_r, got_l = shift(to_l, dx=-1), shift(to_r, dx=1)
    got_r2, got_l2 = shift(to_l2, dx=-1), shift(to_r2, dx=1)
    pooled = after(pooled, to_r)
    pooled = jnp.concatenate([pooled, shift(pooled, mz=1)])
    pooled = jnp.concatenate([pooled, shift(pooled, mz=2)])
    own = own_call(blocks(x_lo, 1, 3, 2, 0), h, h_mean, centred, fc2_weight, fc2_other)
    s1, s3 = add_call(0, 2, own, got_r, got_l)
    t1, t3 = shift(s1, dy=1), shift(s3, dy=-1)
    (s2,) = add_call(2, 1, own, got_r2, got_l2)
    t2 = shift(s2, dy=2)

    owner = pair_owner[:, 0]
    relative = ((owner % 4) ^ z) * 2 + ((owner // 4) ^ x_hi)
    index = (relative * 32 + pair_slot).reshape(32, 1)
    text = text_call(after(index, s2), pooled, text_proj)

    core_index = core.astype(jnp.int32).reshape(1)
    home, e_a, e_b = proj_call(
        core_index, own, got_r2, got_l2, (t1, t2, t3), after(proj_weight, text), proj_other
    )
    s0, s1, s2, s3 = pair_call(home, shift(e_a, dx=-1), shift(e_b, dx=1))
    parts = (s0, shift(s1, dy=1), shift(s2, dy=2), shift(s3, dy=3))
    filtered, weight = last_call(parts, text, threshold)
    return filtered, weight.reshape(32)


def solution(mesh):
    placed = (
        P(("dp", "tensor"), None),
        P(None, "tensor"),
        P("tensor", None),
        P("tensor", None),
        P(("dp", "tensor"), None),
        P(),
        P(("dp", "tensor"), None),
        P(("dp", "tensor")),
        P(),
    )
    return jax.shard_map(
        shards,
        mesh=mesh,
        in_specs=placed,
        out_specs=(P(("dp", "tensor"), None), P(("dp", "tensor"))),
        check_vma=False,
    )
```

```python
import functools

import jax
import jax.numpy as jnp
from jax import lax
from jax.experimental import pallas as pl
from jax.experimental.pallas import tpu as pltpu
from jax.sharding import PartitionSpec as P

eps = 1e-06
sharpness = 40.0
AXES = ("dp", "tensor")
BLK = 640
EW = 1536 + 128
f32 = jnp.float32
bf16 = jnp.bfloat16


def moves(dx=0, dy=0, mz=0, flip=False):
    def place(x, y, z, c):
        return ((x // 2) * 4 + z) * 16 + y * 4 + (x % 2) * 2 + c

    return [
        (place(x, y, z, c), place((x + dx) % 4, (y + dy) % 4, z ^ mz, c ^ int(flip)))
        for x in range(4)
        for y in range(4)
        for z in range(4)
        for c in range(2)
    ]


def shift(value, **step):
    return lax.ppermute(value, AXES, moves(**step))


def after(value, *others):
    return lax.optimization_barrier((value,) + others)[0]


NT = (((1,), (1,)), ((), ()))
TN = (((0,), (0,)), ((), ()))
VM = pl.BlockSpec(memory_space=pltpu.VMEM)
SM = pl.BlockSpec(memory_space=pltpu.SMEM)
HB = pl.BlockSpec(memory_space=pltpu.HBM)


def struct(shape, dtype):
    return jax.ShapeDtypeStruct(shape, dtype)


def call(body, scalars, arrays, outs, scratch=(), remote=0, limit=12, size=1024):
    inside = len(arrays) - remote
    return pl.pallas_call(
        body,
        in_specs=[SM] * len(scalars) + [VM] * inside + [HB] * remote,
        out_specs=(VM,) * len(outs),
        out_shape=outs,
        scratch_shapes=scratch,
        compiler_params=pltpu.CompilerParams(vmem_limit_bytes=limit * 1024 * 1024),
        cost_estimate=pl.CostEstimate(flops=1024, bytes_accessed=size, transcendentals=0),
    )(*scalars, *arrays)


def norm_kernel(cls_ref, normed_ref, centred_ref):
    values = cls_ref[...].astype(f32)
    centred = values - jnp.mean(values, axis=-1, keepdims=True)
    variance = jnp.mean(centred * centred, axis=-1, keepdims=True)
    centred_ref[...] = centred
    normed_ref[...] = (centred * lax.rsqrt(variance + eps)).astype(bf16)


def norm_call(cls_states):
    outs = (struct(cls_states.shape, bf16), struct(cls_states.shape, f32))
    return call(norm_kernel, (), (cls_states,), outs)


def halves_kernel(n0, n1, n2, n3, r_ref, l_ref):
    for k, ref in enumerate((n0, n1, n2, n3)):
        r_ref[16 * k : 16 * k + 16] = ref[:16]
        l_ref[16 * k : 16 * k + 16] = ref[16:]


def halves_call(*ins):
    outs = (struct((64, ins[0].shape[1]), bf16),) * 2
    return call(halves_kernel, (), ins, outs)


def mean_kernel(f_ref, out_ref):
    mean = jnp.sum(f_ref[...].astype(f32), axis=-1, keepdims=True) / f_ref.shape[1]
    high = mean.astype(bf16).astype(f32)
    lane = lax.broadcasted_iota(jnp.int32, out_ref.shape, 1)
    out_ref[...] = jnp.where(lane == 0, high, jnp.where(lane == 1, mean - high, 0.0)).astype(bf16)


def mean_call(f):
    return call(mean_kernel, (), (f,), (struct((f.shape[0], 128), bf16),), size=16 * 1024 * 1024)[0]


def start(copies):
    for copy in copies:
        copy.start()


def wait(copies):
    for copy in copies:
        copy.wait()


def stage_kernel(w_ref, v_ref, out_ref, sems):
    copies = [
        pltpu.make_async_copy(ref.at[pl.ds(at, 400)], out_ref.at[pl.ds(base + at, 400)], sems.at[(base + at) // 400])
        for base, ref in ((0, w_ref), (800, v_ref))
        for at in (0, 400)
    ]
    start(copies)
    wait(copies)


def stage_call(w, v):
    outs = (struct((1600, w.shape[1]), bf16),)
    return call(
        stage_kernel, (), (w, v), outs, [pltpu.SemaphoreType.DMA((4,))], remote=2, limit=4, size=32 * 1024 * 1024
    )[0]


def columns_kernel(cols, f_ref, o_ref, out_ref, sems):
    copies = []
    for q in range(4):
        at = pl.ds(pl.multiple_of(cols[q] * BLK, 128), BLK)
        for k, ref in enumerate((f_ref, o_ref)):
            to = out_ref.at[pl.ds(800 * k, 800), pl.ds(BLK * q, BLK)]
            copies.append(pltpu.make_async_copy(ref.at[:, at], to, sems.at[2 * q + k]))
    start(copies)
    wait(copies)


def columns_call(cols, f, o):
    outs = (struct((1600, 4 * BLK), bf16),)
    return call(
        columns_kernel, (cols,), (f, o), outs, [pltpu.SemaphoreType.DMA((8,))], remote=2, limit=4, size=16 * 1024 * 1024
    )[0]


def fc2_pair(cols, first, h_ref, mean_ref, f_ref, res_ref):
    pair = lax.dot_general(h_ref[...], f_ref[:, BLK * first : BLK * first + 2 * BLK], TN, preferred_element_type=f32)
    for q in range(2):
        part = pair[:, BLK * q : BLK * q + BLK] - mean_ref[:, :1]
        res = res_ref[:, pl.ds(pl.multiple_of(cols[first + q] * BLK, 128), BLK)]
        upper = jnp.concatenate([part[0:16] + res[0:16], part[16:128]], axis=0)
        lower = jnp.concatenate([part[128:192], part[192:208] + res[16:32], part[208:256]], axis=0)
        yield q, upper, lower


def fc1_kernel(w_ref, wm_ref, vm_ref, r, b, a, l, h_ref, mean_ref, rows, sems):
    parts = [pltpu.make_async_copy(ref, rows.at[pl.ds(64 * k, 64)], sems.at[k]) for k, ref in enumerate((r, b, a, l))]
    start(parts)
    wait(parts)
    for at in range(0, 1600, 400):
        z = lax.dot_general(w_ref[at : at + 400], rows[...], NT, preferred_element_type=f32)
        act = 0.5 * z * (1.0 + lax.erf(z * (0.5**0.5)))
        h_ref[at : at + 400] = act.astype(bf16)
    means = lax.dot_general(h_ref[0:800], wm_ref[...], TN, preferred_element_type=f32) + lax.dot_general(
        h_ref[800:1600], vm_ref[...], TN, preferred_element_type=f32
    )
    mean_ref[...] = jnp.broadcast_to(jnp.sum(means, axis=-1, keepdims=True), mean_ref.shape)


def fc1_call(rows, w, w_mean, v_mean):
    outs = (struct((1600, 256), bf16), struct((256, 128), f32))
    return call(
        fc1_kernel,
        (),
        (w, w_mean, v_mean, *rows),
        outs,
        scratch=[pltpu.VMEM((256, w.shape[1]), bf16), pltpu.SemaphoreType.DMA((4,))],
        remote=4,
        limit=10,
    )


def away_kernel(cols, h_ref, mean_ref, res_ref, f_ref, *outs):
    for k in range(2):
        for q, upper, lower in fc2_pair(cols, 2 * k, h_ref, mean_ref, f_ref, res_ref):
            outs[2 * k][q] = upper.astype(bf16)
            outs[2 * k + 1][q] = lower.astype(bf16)


def away_call(cols, h, h_mean, centred, f):
    outs = (struct((2, 128, BLK), bf16),) * 4
    return call(away_kernel, (cols,), (h, h_mean, centred, f), outs, limit=8)


def own_kernel(cols, h_ref, mean_ref, res_ref, f_ref, o_ref, own_ref, buf, sems):
    loads = []
    for q in range(4):
        at = pl.ds(pl.multiple_of(cols[q] * BLK, 128), BLK)
        for k, ref in enumerate((f_ref, o_ref)):
            to = buf.at[pl.ds(800 * k, 800), pl.ds(BLK * q, BLK)]
            loads.append(pltpu.make_async_copy(ref.at[:, at], to, sems.at[2 * q + k]))
    start(loads[:4])
    for k in range(2):
        wait(loads[4 * k : 4 * k + 4])
        if k == 0:
            start(loads[4:])
        for q, upper, lower in fc2_pair(cols, 2 * k, h_ref, mean_ref, buf, res_ref):
            own_ref[2 * k + q, 0:128] = upper
            own_ref[2 * k + q, 128:256] = lower


def own_call(cols, h, h_mean, centred, f, o):
    return call(
        own_kernel,
        (cols,),
        (h, h_mean, centred, f, o),
        (struct((4, 256, BLK), f32),),
        scratch=[pltpu.VMEM((1600, 4 * BLK), bf16), pltpu.SemaphoreType.DMA((8,))],
        remote=2,
        limit=14,
        size=16 * 1024 * 1024,
    )[0]


def add_kernel(place, own_ref, up_ref, low_ref, *outs):
    for k, out in enumerate(outs):
        out[0:128] = (own_ref[place + k, :128] + up_ref[k].astype(f32)).astype(bf16)
        out[128:256] = (own_ref[place + k, 128:] + low_ref[k].astype(f32)).astype(bf16)


def add_call(place, count, own, up, low):
    outs = (struct((256, BLK), bf16),) * count
    return call(functools.partial(add_kernel, place), (), (own, up, low), outs)


def proj_kernel(core, own_ref, up_ref, low_ref, t1, t2, t3, w_ref, o_ref, home_ref, a_ref, b_ref, total, weight):
    weight[pl.ds(pl.multiple_of(core[0] * 320, 64), 320)] = w_ref[...]
    weight[pl.ds(pl.multiple_of((1 - core[0]) * 320, 64), 320)] = o_ref[...]
    total[0:128] = own_ref[3, :128] + up_ref[1].astype(f32)
    total[128:256] = own_ref[3, 128:] + low_ref[1].astype(f32)
    for k, got in ((1, t1), (2, t2), (3, t3)):
        for group in range(4):
            for j in range(4):
                mine = 64 * group + 16 * ((j - k) % 4)
                theirs = 64 * group + 16 * j
                total[mine : mine + 16] += got[theirs : theirs + 16].astype(f32)
    x = total[...]
    squares = jnp.sum(x * x, axis=-1, keepdims=True)
    high = squares.astype(bf16).astype(f32)
    lane = lax.broadcasted_iota(jnp.int32, (256, 128), 1)
    extra = jnp.where(lane == 0, high, jnp.where(lane == 1, squares - high, 0.0)).astype(bf16)
    e = jnp.dot(x.astype(bf16), weight[...], preferred_element_type=f32).astype(bf16)
    for k in range(4):
        for at, base in ((0, 0), (16, 192)):
            src = slice(base + 16 * k, base + 16 * k + 16)
            home_ref[k, at : at + 16, :1536] = e[src]
            home_ref[k, at : at + 16, 1536:] = extra[src]
    b_ref[:, :1536] = e[64:128]
    b_ref[:, 1536:] = extra[64:128]
    a_ref[:, :1536] = e[128:192]
    a_ref[:, 1536:] = extra[128:192]


def proj_call(core, own, up, low, ts, w, o):
    outs = (struct((4, 32, EW), bf16), struct((64, EW), bf16), struct((64, EW), bf16))
    return call(
        proj_kernel,
        (core,),
        (own, up, low, *ts, w, o),
        outs,
        scratch=[pltpu.VMEM((256, BLK), f32), pltpu.VMEM((BLK, 1536), bf16)],
    )


def pair_kernel(home_ref, r_ref, l_ref, s0, s1, s2, s3):
    for k, out in enumerate((s0, s1, s2, s3)):
        at = slice(16 * k, 16 * k + 16)
        out[0:16] = (home_ref[k, 0:16].astype(f32) + r_ref[at].astype(f32)).astype(out.dtype)
        out[16:32] = (home_ref[k, 16:32].astype(f32) + l_ref[at].astype(f32)).astype(out.dtype)


def pair_call(home, r, l):
    outs = (struct((32, EW), f32),) + (struct((32, EW), bf16),) * 3
    return call(pair_kernel, (), (home, r, l), outs)


def text_kernel(index_ref, pooled_ref, proj_ref, out_ref):
    count = pooled_ref.shape[0]
    lane = lax.broadcasted_iota(jnp.int32, (32, count), 1)
    picker = jnp.where(lane == index_ref[...], 1.0, 0.0).astype(bf16)
    values = jnp.dot(picker, pooled_ref[...], preferred_element_type=f32)
    centred = values - jnp.mean(values, axis=-1, keepdims=True)
    variance = jnp.mean(centred * centred, axis=-1, keepdims=True)
    normed = (centred * lax.rsqrt(variance + eps)).astype(bf16)
    u = jnp.dot(normed, proj_ref[...], preferred_element_type=f32)
    out_ref[...] = u * lax.rsqrt(jnp.sum(u * u, axis=-1, keepdims=True) + eps)


def text_call(index, pooled, text_proj):
    outs = (struct((32, text_proj.shape[1]), f32),)
    return call(
        text_kernel, (), (index, pooled, text_proj), outs
    )[0]


def last_kernel(threshold_ref, s0, s1, s2, s3, text_ref, filtered_ref, weight_ref):
    total = s0[...] + s1[...].astype(f32) + s2[...].astype(f32) + s3[...].astype(f32)
    squares = jnp.sum(total[:, 1536:], axis=-1, keepdims=True)
    scale = lax.rsqrt(squares / 5120.0 + eps)
    e = total[:, :1536] * scale
    unit = (e * lax.rsqrt(jnp.sum(e * e, axis=-1, keepdims=True) + eps)).astype(bf16).astype(f32)
    cosine = jnp.sum(unit * text_ref[...], axis=-1, keepdims=True)
    weight = jax.nn.sigmoid(sharpness * (cosine - threshold_ref[0]))
    filtered_ref[...] = (weight * unit).astype(bf16)
    row = lax.broadcasted_iota(jnp.int32, (32, 32), 0)
    column = lax.broadcasted_iota(jnp.int32, (32, 32), 1)
    weight_ref[...] = jnp.sum(jnp.where(row == column, weight, 0.0), axis=0, keepdims=True)


def last_call(parts, text, threshold):
    outs = (struct((32, 1536), bf16), struct((1, 32), f32))
    return call(last_kernel, (threshold,), (*parts, text), outs)


def shards(
    cls_states, fc1_weight, fc2_weight, proj_weight, text_pooled, text_proj, pair_owner, pair_slot, threshold
):
    d = lax.axis_index("dp")
    t = lax.axis_index("tensor")
    x_hi, z, y, x_lo, core = d // 4, d % 4, t // 4, (t // 2) % 2, t % 2

    fc1_rows = fc1_weight.T

    fc1_other = shift(fc1_rows, flip=True)
    normed, centred = norm_call(cls_states)
    n1, n3, n2 = shift(normed, dy=-1), shift(normed, dy=1), shift(normed, dy=2)
    pooled = jnp.concatenate([text_pooled, shift(text_pooled, dx=2)])
    w_mean = mean_call(fc2_weight)
    r, l = halves_call(normed, n1, after(n2, w_mean, pooled), n3)
    a, b = shift(r, dx=1), shift(l, dx=-1)
    fc2_other = shift(after(fc2_weight, r), flip=True)
    v_mean = shift(w_mean, flip=True)
    pooled = after(pooled, r)
    pooled = jnp.concatenate([pooled, shift(pooled, mz=1)])
    pooled_far = shift(pooled, mz=2)
    fc1_both = stage_call(after(fc1_rows, r), fc1_other)

    def blocks(parity, *ks):
        return jnp.stack([2 * ((y + k) % 4) + parity for k in ks]).astype(jnp.int32)

    cols = blocks(1 - x_lo, 1, 3, 2, 0)
    fc2_both = columns_call(cols, fc2_weight, fc2_other)
    h, h_mean = fc1_call((r, after(b, fc2_both), a, l), fc1_both, w_mean, v_mean)
    pooled = jnp.concatenate([pooled, after(pooled_far, h)])
    to_r, to_l, to_r2, to_l2 = away_call(cols, h, h_mean, after(centred, pooled), fc2_both)
    got_r, got_l = shift(to_l, dx=-1), shift(to_r, dx=1)
    got_r2, got_l2 = shift(to_l2, dx=-1), shift(to_r2, dx=1)
    proj_other = shift(after(proj_weight, to_r), flip=True)
    own = own_call(blocks(x_lo, 1, 3, 2, 0), h, h_mean, centred, fc2_weight, fc2_other)
    s1, s3 = add_call(0, 2, own, got_r, got_l)
    t1, t3 = shift(s1, dy=1), shift(s3, dy=-1)
    (s2,) = add_call(2, 1, own, got_r2, got_l2)
    t2 = shift(s2, dy=2)

    owner = pair_owner[:, 0]
    relative = ((owner % 4) ^ z) * 2 + ((owner // 4) ^ x_hi)
    index = (relative * 32 + pair_slot).reshape(32, 1)
    text = text_call(after(index, s2), pooled, text_proj)

    core_index = core.astype(jnp.int32).reshape(1)
    home, e_a, e_b = proj_call(
        core_index, own, got_r2, got_l2, (t1, t2, t3), after(proj_weight, text), proj_other
    )
    s0, s1, s2, s3 = pair_call(home, shift(e_a, dx=-1), shift(e_b, dx=1))
    parts = (s0, shift(s1, dy=1), shift(s2, dy=2), shift(s3, dy=3))
    filtered, weight = last_call(parts, text, threshold)
    return filtered, weight.reshape(32)


def solution(mesh):
    placed = (
        P(("dp", "tensor"), None),
        P(None, "tensor"),
        P("tensor", None),
        P("tensor", None),
        P(("dp", "tensor"), None),
        P(),
        P(("dp", "tensor"), None),
        P(("dp", "tensor")),
        P(),
    )
    return jax.shard_map(
        shards,
        mesh=mesh,
        in_specs=placed,
        out_specs=(P(("dp", "tensor"), None), P(("dp", "tensor"))),
        check_vma=False,
    )
```

```python
import functools

import jax
import jax.numpy as jnp
from jax import lax
from jax.experimental import pallas as pl
from jax.experimental.pallas import tpu as pltpu
from jax.sharding import PartitionSpec as P

eps = 1e-06
sharpness = 40.0
AXES = ("dp", "tensor")
BLK = 640
EW = 1536 + 128
f32 = jnp.float32
bf16 = jnp.bfloat16


def moves(dx=0, dy=0, mz=0, flip=False):
    def place(x, y, z, c):
        return ((x // 2) * 4 + z) * 16 + y * 4 + (x % 2) * 2 + c

    return [
        (place(x, y, z, c), place((x + dx) % 4, (y + dy) % 4, z ^ mz, c ^ int(flip)))
        for x in range(4)
        for y in range(4)
        for z in range(4)
        for c in range(2)
    ]


def shift(value, **step):
    return lax.ppermute(value, AXES, moves(**step))


def after(value, *others):
    return lax.optimization_barrier((value,) + others)[0]


NT = (((1,), (1,)), ((), ()))
TN = (((0,), (0,)), ((), ()))
VM = pl.BlockSpec(memory_space=pltpu.VMEM)
SM = pl.BlockSpec(memory_space=pltpu.SMEM)
HB = pl.BlockSpec(memory_space=pltpu.HBM)


def struct(shape, dtype):
    return jax.ShapeDtypeStruct(shape, dtype)


def call(body, scalars, arrays, outs, scratch=(), remote=0, limit=12, size=1024):
    inside = len(arrays) - remote
    return pl.pallas_call(
        body,
        in_specs=[SM] * len(scalars) + [VM] * inside + [HB] * remote,
        out_specs=(VM,) * len(outs),
        out_shape=outs,
        scratch_shapes=scratch,
        compiler_params=pltpu.CompilerParams(vmem_limit_bytes=limit * 1024 * 1024),
        cost_estimate=pl.CostEstimate(flops=1024, bytes_accessed=size, transcendentals=0),
    )(*scalars, *arrays)


def norm_kernel(cls_ref, normed_ref, centred_ref):
    values = cls_ref[...].astype(f32)
    centred = values - jnp.mean(values, axis=-1, keepdims=True)
    variance = jnp.mean(centred * centred, axis=-1, keepdims=True)
    centred_ref[...] = centred
    normed_ref[...] = (centred * lax.rsqrt(variance + eps)).astype(bf16)


def norm_call(cls_states):
    outs = (struct(cls_states.shape, bf16), struct(cls_states.shape, f32))
    return call(norm_kernel, (), (cls_states,), outs)


def halves_kernel(n0, n1, n2, n3, r_ref, l_ref):
    for k, ref in enumerate((n0, n1, n2, n3)):
        r_ref[16 * k : 16 * k + 16] = ref[:16]
        l_ref[16 * k : 16 * k + 16] = ref[16:]


def halves_call(*ins):
    outs = (struct((64, ins[0].shape[1]), bf16),) * 2
    return call(halves_kernel, (), ins, outs)


def mean_kernel(f_ref, out_ref):
    mean = jnp.sum(f_ref[...].astype(f32), axis=-1, keepdims=True) / f_ref.shape[1]
    high = mean.astype(bf16).astype(f32)
    lane = lax.broadcasted_iota(jnp.int32, out_ref.shape, 1)
    out_ref[...] = jnp.where(lane == 0, high, jnp.where(lane == 1, mean - high, 0.0)).astype(bf16)


def mean_call(f):
    return call(mean_kernel, (), (f,), (struct((f.shape[0], 128), bf16),), size=16 * 1024 * 1024)[0]


def start(copies):
    for copy in copies:
        copy.start()


def wait(copies):
    for copy in copies:
        copy.wait()


def stage_kernel(w_ref, out_ref, sems):
    copies = [
        pltpu.make_async_copy(w_ref.at[pl.ds(at, 400)], out_ref.at[pl.ds(at, 400)], sems.at[at // 400]) for at in (0, 400)
    ]
    start(copies)
    wait(copies)


def stage_call(w):
    outs = (struct(w.shape, bf16),)
    return call(
        stage_kernel, (), (w,), outs, [pltpu.SemaphoreType.DMA((2,))], remote=1, limit=4, size=16 * 1024 * 1024
    )[0]


def columns_kernel(cols, f_ref, o_ref, out_ref, sems):
    copies = []
    for q in range(4):
        at = pl.ds(pl.multiple_of(cols[q] * BLK, 128), BLK)
        for k, ref in enumerate((f_ref, o_ref)):
            to = out_ref.at[pl.ds(800 * k, 800), pl.ds(BLK * q, BLK)]
            copies.append(pltpu.make_async_copy(ref.at[:, at], to, sems.at[2 * q + k]))
    start(copies)
    wait(copies)


def columns_call(cols, f, o):
    outs = (struct((1600, 4 * BLK), bf16),)
    return call(
        columns_kernel, (cols,), (f, o), outs, [pltpu.SemaphoreType.DMA((8,))], remote=2, limit=4, size=16 * 1024 * 1024
    )[0]


def fc2_pair(cols, first, h_ref, mean_ref, f_ref, res_ref):
    pair = lax.dot_general(h_ref[...], f_ref[:, BLK * first : BLK * first + 2 * BLK], TN, preferred_element_type=f32)
    for q in range(2):
        part = pair[:, BLK * q : BLK * q + BLK] - mean_ref[:, :1]
        res = res_ref[:, pl.ds(pl.multiple_of(cols[first + q] * BLK, 128), BLK)]
        upper = jnp.concatenate([part[0:16] + res[0:16], part[16:128]], axis=0)
        lower = jnp.concatenate([part[128:192], part[192:208] + res[16:32], part[208:256]], axis=0)
        yield q, upper, lower


def fc1_kernel(w_ref, v_ref, wm_ref, vm_ref, r, b, a, l, h_ref, mean_ref, rows):
    for k, ref in enumerate((r, b, a, l)):
        rows[64 * k : 64 * k + 64] = ref[...]
    for at in range(0, 1600, 400):
        ref = w_ref if at < 800 else v_ref
        z = lax.dot_general(ref[at % 800 : at % 800 + 400], rows[...], NT, preferred_element_type=f32)
        act = 0.5 * z * (1.0 + lax.erf(z * (0.5**0.5)))
        h_ref[at : at + 400] = act.astype(bf16)
    means = lax.dot_general(h_ref[0:800], wm_ref[...], TN, preferred_element_type=f32) + lax.dot_general(
        h_ref[800:1600], vm_ref[...], TN, preferred_element_type=f32
    )
    mean_ref[...] = jnp.broadcast_to(jnp.sum(means, axis=-1, keepdims=True), mean_ref.shape)


def fc1_call(rows, w, v, w_mean, v_mean):
    outs = (struct((1600, 256), bf16), struct((256, 128), f32))
    return call(
        fc1_kernel,
        (),
        (w, v, w_mean, v_mean, *rows),
        outs,
        scratch=[pltpu.VMEM((256, w.shape[1]), bf16)],
        limit=10,
    )


def away_kernel(cols, h_ref, mean_ref, res_ref, f_ref, *outs):
    for k in range(2):
        for q, upper, lower in fc2_pair(cols, 2 * k, h_ref, mean_ref, f_ref, res_ref):
            outs[2 * k][q] = upper.astype(bf16)
            outs[2 * k + 1][q] = lower.astype(bf16)


def away_call(cols, h, h_mean, centred, f):
    outs = (struct((2, 128, BLK), bf16),) * 4
    return call(away_kernel, (cols,), (h, h_mean, centred, f), outs, limit=8)


def own_kernel(cols, h_ref, mean_ref, res_ref, f_ref, o_ref, own_ref, buf, sems):
    loads = []
    for q in range(4):
        at = pl.ds(pl.multiple_of(cols[q] * BLK, 128), BLK)
        for k, ref in enumerate((f_ref, o_ref)):
            to = buf.at[pl.ds(800 * k, 800), pl.ds(BLK * q, BLK)]
            loads.append(pltpu.make_async_copy(ref.at[:, at], to, sems.at[2 * q + k]))
    start(loads[:4])
    for k in range(2):
        wait(loads[4 * k : 4 * k + 4])
        if k == 0:
            start(loads[4:])
        for q, upper, lower in fc2_pair(cols, 2 * k, h_ref, mean_ref, buf, res_ref):
            own_ref[2 * k + q, 0:128] = upper
            own_ref[2 * k + q, 128:256] = lower


def own_call(cols, h, h_mean, centred, f, o):
    return call(
        own_kernel,
        (cols,),
        (h, h_mean, centred, f, o),
        (struct((4, 256, BLK), f32),),
        scratch=[pltpu.VMEM((1600, 4 * BLK), bf16), pltpu.SemaphoreType.DMA((8,))],
        remote=2,
        limit=14,
        size=16 * 1024 * 1024,
    )[0]


def add_kernel(place, own_ref, up_ref, low_ref, *outs):
    for k, out in enumerate(outs):
        out[0:128] = (own_ref[place + k, :128] + up_ref[k].astype(f32)).astype(bf16)
        out[128:256] = (own_ref[place + k, 128:] + low_ref[k].astype(f32)).astype(bf16)


def add_call(place, count, own, up, low):
    outs = (struct((256, BLK), bf16),) * count
    return call(functools.partial(add_kernel, place), (), (own, up, low), outs)


def proj_kernel(core, own_ref, up_ref, low_ref, t1, t2, t3, w_ref, o_ref, home_ref, a_ref, b_ref, total, weight):
    weight[pl.ds(pl.multiple_of(core[0] * 320, 64), 320)] = w_ref[...]
    weight[pl.ds(pl.multiple_of((1 - core[0]) * 320, 64), 320)] = o_ref[...]
    total[0:128] = own_ref[3, :128] + up_ref[1].astype(f32)
    total[128:256] = own_ref[3, 128:] + low_ref[1].astype(f32)
    for k, got in ((1, t1), (2, t2), (3, t3)):
        for group in range(4):
            for j in range(4):
                mine = 64 * group + 16 * ((j - k) % 4)
                theirs = 64 * group + 16 * j
                total[mine : mine + 16] += got[theirs : theirs + 16].astype(f32)
    x = total[...]
    squares = jnp.sum(x * x, axis=-1, keepdims=True)
    high = squares.astype(bf16).astype(f32)
    lane = lax.broadcasted_iota(jnp.int32, (256, 128), 1)
    extra = jnp.where(lane == 0, high, jnp.where(lane == 1, squares - high, 0.0)).astype(bf16)
    e = jnp.dot(x.astype(bf16), weight[...], preferred_element_type=f32).astype(bf16)
    for k in range(4):
        for at, base in ((0, 0), (16, 192)):
            src = slice(base + 16 * k, base + 16 * k + 16)
            home_ref[k, at : at + 16, :1536] = e[src]
            home_ref[k, at : at + 16, 1536:] = extra[src]
    b_ref[:, :1536] = e[64:128]
    b_ref[:, 1536:] = extra[64:128]
    a_ref[:, :1536] = e[128:192]
    a_ref[:, 1536:] = extra[128:192]


def proj_call(core, own, up, low, ts, w, o):
    outs = (struct((4, 32, EW), bf16), struct((64, EW), bf16), struct((64, EW), bf16))
    return call(
        proj_kernel,
        (core,),
        (own, up, low, *ts, w, o),
        outs,
        scratch=[pltpu.VMEM((256, BLK), f32), pltpu.VMEM((BLK, 1536), bf16)],
    )


def pair_kernel(home_ref, r_ref, l_ref, s0, s1, s2, s3):
    for k, out in enumerate((s0, s1, s2, s3)):
        at = slice(16 * k, 16 * k + 16)
        out[0:16] = (home_ref[k, 0:16].astype(f32) + r_ref[at].astype(f32)).astype(out.dtype)
        out[16:32] = (home_ref[k, 16:32].astype(f32) + l_ref[at].astype(f32)).astype(out.dtype)


def pair_call(home, r, l):
    outs = (struct((32, EW), f32),) + (struct((32, EW), bf16),) * 3
    return call(pair_kernel, (), (home, r, l), outs)


def text_kernel(index_ref, pooled_ref, proj_ref, out_ref):
    count = pooled_ref.shape[0]
    lane = lax.broadcasted_iota(jnp.int32, (32, count), 1)
    picker = jnp.where(lane == index_ref[...], 1.0, 0.0).astype(bf16)
    values = jnp.dot(picker, pooled_ref[...], preferred_element_type=f32)
    centred = values - jnp.mean(values, axis=-1, keepdims=True)
    variance = jnp.mean(centred * centred, axis=-1, keepdims=True)
    normed = (centred * lax.rsqrt(variance + eps)).astype(bf16)
    u = jnp.dot(normed, proj_ref[...], preferred_element_type=f32)
    out_ref[...] = u * lax.rsqrt(jnp.sum(u * u, axis=-1, keepdims=True) + eps)


def text_call(index, pooled, text_proj):
    outs = (struct((32, text_proj.shape[1]), f32),)
    return call(
        text_kernel, (), (index, pooled, text_proj), outs
    )[0]


def last_kernel(threshold_ref, s0, s1, s2, s3, text_ref, filtered_ref, weight_ref):
    total = s0[...] + s1[...].astype(f32) + s2[...].astype(f32) + s3[...].astype(f32)
    squares = jnp.sum(total[:, 1536:], axis=-1, keepdims=True)
    scale = lax.rsqrt(squares / 5120.0 + eps)
    e = total[:, :1536] * scale
    unit = (e * lax.rsqrt(jnp.sum(e * e, axis=-1, keepdims=True) + eps)).astype(bf16).astype(f32)
    cosine = jnp.sum(unit * text_ref[...], axis=-1, keepdims=True)
    weight = jax.nn.sigmoid(sharpness * (cosine - threshold_ref[0]))
    filtered_ref[...] = (weight * unit).astype(bf16)
    row = lax.broadcasted_iota(jnp.int32, (32, 32), 0)
    column = lax.broadcasted_iota(jnp.int32, (32, 32), 1)
    weight_ref[...] = jnp.sum(jnp.where(row == column, weight, 0.0), axis=0, keepdims=True)


def last_call(parts, text, threshold):
    outs = (struct((32, 1536), bf16), struct((1, 32), f32))
    return call(last_kernel, (threshold,), (*parts, text), outs)


def shards(
    cls_states, fc1_weight, fc2_weight, proj_weight, text_pooled, text_proj, pair_owner, pair_slot, threshold
):
    d = lax.axis_index("dp")
    t = lax.axis_index("tensor")
    x_hi, z, y, x_lo, core = d // 4, d % 4, t // 4, (t // 2) % 2, t % 2

    fc1_rows = fc1_weight.T

    fc1_other = shift(fc1_rows, flip=True)
    normed, centred = norm_call(cls_states)
    n1, n3, n2 = shift(normed, dy=-1), shift(normed, dy=1), shift(normed, dy=2)
    pooled = jnp.concatenate([text_pooled, shift(text_pooled, dx=2)])
    w_mean = mean_call(fc2_weight)
    fc1_near = stage_call(after(fc1_rows, w_mean))
    r, l = halves_call(normed, n1, after(n2, w_mean, pooled, fc1_near), n3)
    a, b = shift(r, dx=1), shift(l, dx=-1)
    fc2_other = shift(after(fc2_weight, r), flip=True)
    v_mean = shift(w_mean, flip=True)
    pooled = after(pooled, r)
    pooled = jnp.concatenate([pooled, shift(pooled, mz=1)])
    pooled_far = shift(pooled, mz=2)
    fc1_far = stage_call(fc1_other)

    def blocks(parity, *ks):
        return jnp.stack([2 * ((y + k) % 4) + parity for k in ks]).astype(jnp.int32)

    cols = blocks(1 - x_lo, 1, 3, 2, 0)
    fc2_both = columns_call(cols, fc2_weight, fc2_other)
    h, h_mean = fc1_call((r, after(b, fc2_both), a, l), fc1_near, fc1_far, w_mean, v_mean)
    pooled = jnp.concatenate([pooled, after(pooled_far, h)])
    to_r, to_l, to_r2, to_l2 = away_call(cols, h, h_mean, after(centred, pooled), fc2_both)
    got_r, got_l = shift(to_l, dx=-1), shift(to_r, dx=1)
    got_r2, got_l2 = shift(to_l2, dx=-1), shift(to_r2, dx=1)
    proj_other = shift(after(proj_weight, to_r), flip=True)
    own = own_call(blocks(x_lo, 1, 3, 2, 0), h, h_mean, centred, fc2_weight, fc2_other)
    s1, s3 = add_call(0, 2, own, got_r, got_l)
    t1, t3 = shift(s1, dy=1), shift(s3, dy=-1)
    (s2,) = add_call(2, 1, own, got_r2, got_l2)
    t2 = shift(s2, dy=2)

    owner = pair_owner[:, 0]
    relative = ((owner % 4) ^ z) * 2 + ((owner // 4) ^ x_hi)
    index = (relative * 32 + pair_slot).reshape(32, 1)
    text = text_call(after(index, s2), pooled, text_proj)

    core_index = core.astype(jnp.int32).reshape(1)
    home, e_a, e_b = proj_call(
        core_index, own, got_r2, got_l2, (t1, t2, t3), after(proj_weight, text), proj_other
    )
    s0, s1, s2, s3 = pair_call(home, shift(e_a, dx=-1), shift(e_b, dx=1))
    parts = (s0, shift(s1, dy=1), shift(s2, dy=2), shift(s3, dy=3))
    filtered, weight = last_call(parts, text, threshold)
    return filtered, weight.reshape(32)


def solution(mesh):
    placed = (
        P(("dp", "tensor"), None),
        P(None, "tensor"),
        P("tensor", None),
        P("tensor", None),
        P(("dp", "tensor"), None),
        P(),
        P(("dp", "tensor"), None),
        P(("dp", "tensor")),
        P(),
    )
    return jax.shard_map(
        shards,
        mesh=mesh,
        in_specs=placed,
        out_specs=(P(("dp", "tensor"), None), P(("dp", "tensor"))),
        check_vma=False,
    )
```

```python
import functools

import jax
import jax.numpy as jnp
from jax import lax
from jax.experimental import pallas as pl
from jax.experimental.pallas import tpu as pltpu
from jax.sharding import PartitionSpec as P

eps = 1e-06
sharpness = 40.0
AXES = ("dp", "tensor")
BLK = 640
EW = 1536 + 128
f32 = jnp.float32
bf16 = jnp.bfloat16


def moves(dx=0, dy=0, mz=0, flip=False):
    def place(x, y, z, c):
        return ((x // 2) * 4 + z) * 16 + y * 4 + (x % 2) * 2 + c

    return [
        (place(x, y, z, c), place((x + dx) % 4, (y + dy) % 4, z ^ mz, c ^ int(flip)))
        for x in range(4)
        for y in range(4)
        for z in range(4)
        for c in range(2)
    ]


def shift(value, **step):
    return lax.ppermute(value, AXES, moves(**step))


def after(value, *others):
    return lax.optimization_barrier((value,) + others)[0]


NT = (((1,), (1,)), ((), ()))
TN = (((0,), (0,)), ((), ()))
VM = pl.BlockSpec(memory_space=pltpu.VMEM)
SM = pl.BlockSpec(memory_space=pltpu.SMEM)
HB = pl.BlockSpec(memory_space=pltpu.HBM)


def struct(shape, dtype):
    return jax.ShapeDtypeStruct(shape, dtype)


def call(body, scalars, arrays, outs, scratch=(), remote=0, limit=12, size=1024):
    inside = len(arrays) - remote
    return pl.pallas_call(
        body,
        in_specs=[SM] * len(scalars) + [VM] * inside + [HB] * remote,
        out_specs=(VM,) * len(outs),
        out_shape=outs,
        scratch_shapes=scratch,
        compiler_params=pltpu.CompilerParams(vmem_limit_bytes=limit * 1024 * 1024),
        cost_estimate=pl.CostEstimate(flops=1024, bytes_accessed=size, transcendentals=0),
    )(*scalars, *arrays)


def norm_kernel(cls_ref, normed_ref, centred_ref):
    values = cls_ref[...].astype(f32)
    centred = values - jnp.mean(values, axis=-1, keepdims=True)
    variance = jnp.mean(centred * centred, axis=-1, keepdims=True)
    centred_ref[...] = centred
    normed_ref[...] = (centred * lax.rsqrt(variance + eps)).astype(bf16)


def norm_call(cls_states):
    outs = (struct(cls_states.shape, bf16), struct(cls_states.shape, f32))
    return call(norm_kernel, (), (cls_states,), outs)


def halves_kernel(n0, n1, n2, n3, r_ref, l_ref):
    for k, ref in enumerate((n0, n1, n2, n3)):
        r_ref[16 * k : 16 * k + 16] = ref[:16]
        l_ref[16 * k : 16 * k + 16] = ref[16:]


def halves_call(*ins):
    outs = (struct((64, ins[0].shape[1]), bf16),) * 2
    return call(halves_kernel, (), ins, outs)


def mean_kernel(f_ref, out_ref):
    mean = jnp.sum(f_ref[...].astype(f32), axis=-1, keepdims=True) / f_ref.shape[1]
    high = mean.astype(bf16).astype(f32)
    lane = lax.broadcasted_iota(jnp.int32, out_ref.shape, 1)
    out_ref[...] = jnp.where(lane == 0, high, jnp.where(lane == 1, mean - high, 0.0)).astype(bf16)


def mean_call(f):
    return call(mean_kernel, (), (f,), (struct((f.shape[0], 128), bf16),), size=16 * 1024 * 1024)[0]


def start(copies):
    for copy in copies:
        copy.start()


def wait(copies):
    for copy in copies:
        copy.wait()


def stage_kernel(w_ref, out_ref, sems):
    copies = [
        pltpu.make_async_copy(w_ref.at[pl.ds(at, 400)], out_ref.at[pl.ds(at, 400)], sems.at[at // 400]) for at in (0, 400)
    ]
    start(copies)
    wait(copies)


def stage_call(w):
    outs = (struct(w.shape, bf16),)
    return call(
        stage_kernel, (), (w,), outs, [pltpu.SemaphoreType.DMA((2,))], remote=1, limit=4, size=16 * 1024 * 1024
    )[0]


def columns_kernel(cols, f_ref, o_ref, out_ref, sems):
    copies = []
    for q in range(4):
        at = pl.ds(pl.multiple_of(cols[q] * BLK, 128), BLK)
        for k, ref in enumerate((f_ref, o_ref)):
            to = out_ref.at[pl.ds(800 * k, 800), pl.ds(BLK * q, BLK)]
            copies.append(pltpu.make_async_copy(ref.at[:, at], to, sems.at[2 * q + k]))
    start(copies)
    wait(copies)


def columns_call(cols, f, o):
    outs = (struct((1600, 4 * BLK), bf16),)
    return call(
        columns_kernel, (cols,), (f, o), outs, [pltpu.SemaphoreType.DMA((8,))], remote=2, limit=4, size=16 * 1024 * 1024
    )[0]


def fc2_pair(cols, first, h_ref, mean_ref, f_ref, res_ref):
    pair = lax.dot_general(h_ref[...], f_ref[:, BLK * first : BLK * first + 2 * BLK], TN, preferred_element_type=f32)
    for q in range(2):
        part = pair[:, BLK * q : BLK * q + BLK] - mean_ref[:, :1]
        res = res_ref[:, pl.ds(pl.multiple_of(cols[first + q] * BLK, 128), BLK)]
        upper = jnp.concatenate([part[0:16] + res[0:16], part[16:128]], axis=0)
        lower = jnp.concatenate([part[128:192], part[192:208] + res[16:32], part[208:256]], axis=0)
        yield q, upper, lower


def fc1_kernel(w_ref, v_ref, wm_ref, vm_ref, r, b, a, l, h_ref, mean_ref, rows):
    for k, ref in enumerate((r, b, a, l)):
        rows[64 * k : 64 * k + 64] = ref[...]
    for at in range(0, 1600, 400):
        ref = w_ref if at < 800 else v_ref
        z = lax.dot_general(ref[at % 800 : at % 800 + 400], rows[...], NT, preferred_element_type=f32)
        act = 0.5 * z * (1.0 + lax.erf(z * (0.5**0.5)))
        h_ref[at : at + 400] = act.astype(bf16)
    means = lax.dot_general(h_ref[0:800], wm_ref[...], TN, preferred_element_type=f32) + lax.dot_general(
        h_ref[800:1600], vm_ref[...], TN, preferred_element_type=f32
    )
    mean_ref[...] = jnp.broadcast_to(jnp.sum(means, axis=-1, keepdims=True), mean_ref.shape)


def fc1_call(rows, w, v, w_mean, v_mean):
    outs = (struct((1600, 256), bf16), struct((256, 128), f32))
    return call(
        fc1_kernel,
        (),
        (w, v, w_mean, v_mean, *rows),
        outs,
        scratch=[pltpu.VMEM((256, w.shape[1]), bf16)],
        limit=10,
    )


def away_kernel(cols, h_ref, mean_ref, res_ref, f_ref, *outs):
    for k in range(2):
        for q, upper, lower in fc2_pair(cols, 2 * k, h_ref, mean_ref, f_ref, res_ref):
            outs[2 * k][q] = upper.astype(bf16)
            outs[2 * k + 1][q] = lower.astype(bf16)


def away_call(cols, h, h_mean, centred, f):
    outs = (struct((2, 128, BLK), bf16),) * 4
    return call(away_kernel, (cols,), (h, h_mean, centred, f), outs, limit=8)


def own_kernel(cols, h_ref, mean_in, res_in, f_ref, o_ref, own_ref, buf, mean_ref, res_ref, sems):
    small = [
        pltpu.make_async_copy(mean_in, mean_ref, sems.at[8]),
        pltpu.make_async_copy(res_in, res_ref, sems.at[9]),
    ]
    start(small)
    loads = []
    for q in range(4):
        at = pl.ds(pl.multiple_of(cols[q] * BLK, 128), BLK)
        for k, ref in enumerate((f_ref, o_ref)):
            to = buf.at[pl.ds(800 * k, 800), pl.ds(BLK * q, BLK)]
            loads.append(pltpu.make_async_copy(ref.at[:, at], to, sems.at[2 * q + k]))
    start(loads[:4])
    wait(small)
    for k in range(2):
        wait(loads[4 * k : 4 * k + 4])
        if k == 0:
            start(loads[4:])
        for q, upper, lower in fc2_pair(cols, 2 * k, h_ref, mean_ref, buf, res_ref):
            own_ref[2 * k + q, 0:128] = upper
            own_ref[2 * k + q, 128:256] = lower


def own_call(cols, h, h_mean, centred, f, o):
    return call(
        own_kernel,
        (cols,),
        (h, h_mean, centred, f, o),
        (struct((4, 256, BLK), f32),),
        scratch=[
            pltpu.VMEM((1600, 4 * BLK), bf16),
            pltpu.VMEM(h_mean.shape, f32),
            pltpu.VMEM(centred.shape, f32),
            pltpu.SemaphoreType.DMA((10,)),
        ],
        remote=4,
        limit=14,
        size=16 * 1024 * 1024,
    )[0]


def add_kernel(place, own_ref, up_ref, low_ref, *outs):
    for k, out in enumerate(outs):
        out[0:128] = (own_ref[place + k, :128] + up_ref[k].astype(f32)).astype(bf16)
        out[128:256] = (own_ref[place + k, 128:] + low_ref[k].astype(f32)).astype(bf16)


def add_call(place, count, own, up, low):
    outs = (struct((256, BLK), bf16),) * count
    return call(functools.partial(add_kernel, place), (), (own, up, low), outs)


def proj_kernel(core, own_ref, up_ref, low_ref, t1, t2, t3, w_ref, o_ref, home_ref, a_ref, b_ref, total, weight):
    weight[pl.ds(pl.multiple_of(core[0] * 320, 64), 320)] = w_ref[...]
    weight[pl.ds(pl.multiple_of((1 - core[0]) * 320, 64), 320)] = o_ref[...]
    total[0:128] = own_ref[3, :128] + up_ref[1].astype(f32)
    total[128:256] = own_ref[3, 128:] + low_ref[1].astype(f32)
    for k, got in ((1, t1), (2, t2), (3, t3)):
        for group in range(4):
            for j in range(4):
                mine = 64 * group + 16 * ((j - k) % 4)
                theirs = 64 * group + 16 * j
                total[mine : mine + 16] += got[theirs : theirs + 16].astype(f32)
    x = total[...]
    squares = jnp.sum(x * x, axis=-1, keepdims=True)
    high = squares.astype(bf16).astype(f32)
    lane = lax.broadcasted_iota(jnp.int32, (256, 128), 1)
    extra = jnp.where(lane == 0, high, jnp.where(lane == 1, squares - high, 0.0)).astype(bf16)
    e = jnp.dot(x.astype(bf16), weight[...], preferred_element_type=f32).astype(bf16)
    for k in range(4):
        for at, base in ((0, 0), (16, 192)):
            src = slice(base + 16 * k, base + 16 * k + 16)
            home_ref[k, at : at + 16, :1536] = e[src]
            home_ref[k, at : at + 16, 1536:] = extra[src]
    b_ref[:, :1536] = e[64:128]
    b_ref[:, 1536:] = extra[64:128]
    a_ref[:, :1536] = e[128:192]
    a_ref[:, 1536:] = extra[128:192]


def proj_call(core, own, up, low, ts, w, o):
    outs = (struct((4, 32, EW), bf16), struct((64, EW), bf16), struct((64, EW), bf16))
    return call(
        proj_kernel,
        (core,),
        (own, up, low, *ts, w, o),
        outs,
        scratch=[pltpu.VMEM((256, BLK), f32), pltpu.VMEM((BLK, 1536), bf16)],
    )


def pair_kernel(home_ref, r_ref, l_ref, s0, s1, s2, s3):
    for k, out in enumerate((s0, s1, s2, s3)):
        at = slice(16 * k, 16 * k + 16)
        out[0:16] = (home_ref[k, 0:16].astype(f32) + r_ref[at].astype(f32)).astype(out.dtype)
        out[16:32] = (home_ref[k, 16:32].astype(f32) + l_ref[at].astype(f32)).astype(out.dtype)


def pair_call(home, r, l):
    outs = (struct((32, EW), f32),) + (struct((32, EW), bf16),) * 3
    return call(pair_kernel, (), (home, r, l), outs)


def text_kernel(index_ref, pooled_ref, proj_ref, out_ref):
    count = pooled_ref.shape[0]
    lane = lax.broadcasted_iota(jnp.int32, (32, count), 1)
    picker = jnp.where(lane == index_ref[...], 1.0, 0.0).astype(bf16)
    values = jnp.dot(picker, pooled_ref[...], preferred_element_type=f32)
    centred = values - jnp.mean(values, axis=-1, keepdims=True)
    variance = jnp.mean(centred * centred, axis=-1, keepdims=True)
    normed = (centred * lax.rsqrt(variance + eps)).astype(bf16)
    u = jnp.dot(normed, proj_ref[...], preferred_element_type=f32)
    out_ref[...] = u * lax.rsqrt(jnp.sum(u * u, axis=-1, keepdims=True) + eps)


def text_call(index, pooled, text_proj):
    outs = (struct((32, text_proj.shape[1]), f32),)
    return call(
        text_kernel, (), (index, pooled, text_proj), outs
    )[0]


def last_kernel(threshold_ref, s0, s1, s2, s3, text_ref, filtered_ref, weight_ref):
    total = s0[...] + s1[...].astype(f32) + s2[...].astype(f32) + s3[...].astype(f32)
    squares = jnp.sum(total[:, 1536:], axis=-1, keepdims=True)
    scale = lax.rsqrt(squares / 5120.0 + eps)
    e = total[:, :1536] * scale
    unit = (e * lax.rsqrt(jnp.sum(e * e, axis=-1, keepdims=True) + eps)).astype(bf16).astype(f32)
    cosine = jnp.sum(unit * text_ref[...], axis=-1, keepdims=True)
    weight = jax.nn.sigmoid(sharpness * (cosine - threshold_ref[0]))
    filtered_ref[...] = (weight * unit).astype(bf16)
    row = lax.broadcasted_iota(jnp.int32, (32, 32), 0)
    column = lax.broadcasted_iota(jnp.int32, (32, 32), 1)
    weight_ref[...] = jnp.sum(jnp.where(row == column, weight, 0.0), axis=0, keepdims=True)


def last_call(parts, text, threshold):
    outs = (struct((32, 1536), bf16), struct((1, 32), f32))
    return call(last_kernel, (threshold,), (*parts, text), outs)


def shards(
    cls_states, fc1_weight, fc2_weight, proj_weight, text_pooled, text_proj, pair_owner, pair_slot, threshold
):
    d = lax.axis_index("dp")
    t = lax.axis_index("tensor")
    x_hi, z, y, x_lo, core = d // 4, d % 4, t // 4, (t // 2) % 2, t % 2

    fc1_rows = fc1_weight.T

    fc1_other = shift(fc1_rows, flip=True)
    normed, centred = norm_call(cls_states)
    n1, n3, n2 = shift(normed, dy=-1), shift(normed, dy=1), shift(normed, dy=2)
    pooled = jnp.concatenate([text_pooled, shift(text_pooled, dx=2)])
    w_mean = mean_call(fc2_weight)
    fc1_near = stage_call(after(fc1_rows, w_mean))
    r, l = halves_call(normed, n1, after(n2, w_mean, pooled, fc1_near), n3)
    a, b = shift(r, dx=1), shift(l, dx=-1)
    fc2_other = shift(after(fc2_weight, r), flip=True)
    v_mean = shift(w_mean, flip=True)
    pooled = after(pooled, r)
    pooled = jnp.concatenate([pooled, shift(pooled, mz=1)])
    pooled_far = shift(pooled, mz=2)
    fc1_far = stage_call(fc1_other)

    def blocks(parity, *ks):
        return jnp.stack([2 * ((y + k) % 4) + parity for k in ks]).astype(jnp.int32)

    cols = blocks(1 - x_lo, 1, 3, 2, 0)
    fc2_both = columns_call(cols, fc2_weight, fc2_other)
    h, h_mean = fc1_call((r, after(b, fc2_both), a, l), fc1_near, fc1_far, w_mean, v_mean)
    pooled = jnp.concatenate([pooled, after(pooled_far, h)])
    to_r, to_l, to_r2, to_l2 = away_call(cols, h, h_mean, after(centred, pooled), fc2_both)
    got_r, got_l = shift(to_l, dx=-1), shift(to_r, dx=1)
    got_r2, got_l2 = shift(to_l2, dx=-1), shift(to_r2, dx=1)
    proj_other = shift(after(proj_weight, to_r), flip=True)
    own = own_call(blocks(x_lo, 1, 3, 2, 0), h, h_mean, centred, fc2_weight, fc2_other)
    s1, s3 = add_call(0, 2, own, got_r, got_l)
    t1, t3 = shift(s1, dy=1), shift(s3, dy=-1)
    (s2,) = add_call(2, 1, own, got_r2, got_l2)
    t2 = shift(s2, dy=2)

    owner = pair_owner[:, 0]
    relative = ((owner % 4) ^ z) * 2 + ((owner // 4) ^ x_hi)
    index = (relative * 32 + pair_slot).reshape(32, 1)
    text = text_call(after(index, s2), pooled, text_proj)

    core_index = core.astype(jnp.int32).reshape(1)
    home, e_a, e_b = proj_call(
        core_index, own, got_r2, got_l2, (t1, t2, t3), after(proj_weight, text), proj_other
    )
    s0, s1, s2, s3 = pair_call(home, shift(e_a, dx=-1), shift(e_b, dx=1))
    parts = (s0, shift(s1, dy=1), shift(s2, dy=2), shift(s3, dy=3))
    filtered, weight = last_call(parts, text, threshold)
    return filtered, weight.reshape(32)


def solution(mesh):
    placed = (
        P(("dp", "tensor"), None),
        P(None, "tensor"),
        P("tensor", None),
        P("tensor", None),
        P(("dp", "tensor"), None),
        P(),
        P(("dp", "tensor"), None),
        P(("dp", "tensor")),
        P(),
    )
    return jax.shard_map(
        shards,
        mesh=mesh,
        in_specs=placed,
        out_specs=(P(("dp", "tensor"), None), P(("dp", "tensor"))),
        check_vma=False,
    )
```
